512 devices in a mesh: aa: 8 (over z), ba: 16 (over y, core), col: 4 (over x).
Axes of the slice: x: 4, y: 8, z: 8, core: 2. Of those that a mesh axis runs over, the one named last changes fastest.
Arguments:
- tensor: bfloat16 [512, 512, 512], P('aa', 'ba', 'col'), may hold values from -24 to 24
- factor_b_init: float32 [512, 256], P(('ba', 'aa', 'col')), may hold values from -5.2 to 6.8
- factor_c_init: float32 [512, 256], P(('col', 'aa', 'ba')), may hold values from -5.2 to 6.8
Outputs:
- factor_a: float32 [512, 256], P(('aa', 'ba', 'col'))
- factor_b: float32 [512, 256], P(('ba', 'aa', 'col'))
- factor_c: float32 [512, 256], P(('col', 'aa', 'ba'))
The draws below stay inside these ranges and needn't reach their ends.
All inputs are finite; a program needn't handle non-finite values.
Results may differ from the reference program's by a relative error of at most 0.007.
The reference program's roundings to bfloat16 on the way (of `c_low` and `a_low`) count: a program that leaves them out, or rounds other values in their place, can miss the bound.
Values may be sent and summed in bfloat16 or wider, within the bound.
No kernel may reach another device: no remote copies, remote signals or barrier semaphores. Data moves between devices by JAX's collectives and lax.ppermute only.
A program may use at most 64 MiB of HBM per device.

```python
import jax
import jax.numpy as jnp
from jax import lax

BLK_I = 64
BLK_K = 128
RANK = 256
DIM_I = 512
DIM_J = 512
DIM_K = 512
N_AA = 8
N_COL = 4


def rising(length):
    return 1.0 + jnp.arange(length, dtype=jnp.float32) / max(length - 1, 1)


def draw_tensor(key, part):
    base = jnp.clip(jax.random.normal(key, (DIM_I, DIM_J, DIM_K), jnp.float32), -3.0, 3.0)
    frames = jnp.exp(jax.random.uniform(jax.random.fold_in(key, 11), (DIM_K,), jnp.float32, jnp.log(0.25), 0.0))
    scaled = base * rising(DIM_I)[:, None, None] * rising(DIM_J)[None, :, None]
    return (scaled * (rising(DIM_K) * frames)[None, None, :]).astype(jnp.bfloat16)


def factor_draw(key, length):
    base = 0.4 + jnp.clip(jax.random.normal(key, (length, RANK), jnp.float32), -3.0, 3.0)
    row_scale = jnp.exp(jax.random.uniform(jax.random.fold_in(key, 7), (length,), jnp.float32, jnp.log(0.25), 0.0))
    return base * (rising(length) * row_scale)[:, None]


def draw_factor_b_init(key, part):
    return factor_draw(jax.random.fold_in(key, 21), DIM_J)


def draw_factor_c_init(key, part):
    return factor_draw(jax.random.fold_in(key, 31), DIM_K)


def setup_inputs(seed: int = 0) -> dict:
    splits = jax.random.split(jax.random.key(seed), 4)
    tensor = draw_tensor(jax.random.fold_in(splits[3], 71), 0)
    factor_b_init = draw_factor_b_init(jax.random.fold_in(splits[3], 71), 0)
    factor_c_init = draw_factor_c_init(jax.random.fold_in(splits[3], 71), 0)
    return dict(tensor=tensor, factor_b_init=factor_b_init, factor_c_init=factor_c_init)


EPSILON = 1e-06
HIGHEST = lax.Precision.HIGHEST

def gram_of(rows):
    return jnp.dot(rows.T.astype(jnp.float32), rows.astype(jnp.float32), precision=HIGHEST, preferred_element_type=jnp.float32)

def solve_rows(products, left_gram, right_gram):
    lower = jnp.linalg.cholesky(left_gram * right_gram)
    return jax.scipy.linalg.cho_solve((lower, True), products.T).T

def normalize(raw_rows, total_rows):
    scale = jnp.sqrt(lax.optimization_barrier(jnp.sum(raw_rows * raw_rows, axis=0)) / total_rows + EPSILON)
    return raw_rows / scale

def reference(tensor, factor_b_init, factor_c_init):
    c_low = lax.optimization_barrier(factor_c_init.astype(jnp.bfloat16)).astype(jnp.float32)
    gram_b = gram_of(factor_b_init)
    gram_c = gram_of(factor_c_init)
    tensor_rows = tensor.reshape(N_AA, BLK_I, DIM_J, DIM_K)

    def contract_frames(block):
        return jnp.einsum('ijk,kr->ijr', block.astype(jnp.float32), c_low, precision=HIGHEST)

    def first_mode(block):
        inner = contract_frames(block)
        return jnp.einsum('ijr,jr->ir', inner, factor_b_init, precision=HIGHEST)
    mttkrp_a = lax.map(first_mode, tensor_rows).reshape(DIM_I, RANK)
    factor_a = normalize(solve_rows(mttkrp_a, gram_b, gram_c), DIM_I)
    gram_a = gram_of(factor_a)
    a_blocks = factor_a.reshape(N_AA, BLK_I, RANK)

    def second_mode(total, pair):
        block, a_rows = pair
        inner = contract_frames(block)
        return (total + jnp.einsum('ijr,ir->jr', inner, a_rows, precision=HIGHEST), None)
    mttkrp_b, _ = lax.scan(second_mode, jnp.zeros((DIM_J, RANK), jnp.float32), (tensor_rows, a_blocks))
    factor_b = normalize(solve_rows(mttkrp_b, gram_a, gram_c), DIM_J)
    gram_b_new = gram_of(factor_b)
    a_low = lax.optimization_barrier(factor_a.astype(jnp.bfloat16)).astype(jnp.float32)

    def third_mode(index):
        block = lax.dynamic_slice_in_dim(tensor, (index * BLK_K).astype(jnp.int32), BLK_K, 2).astype(jnp.float32)
        inner = jnp.einsum('ijk,ir->jkr', block, a_low, precision=HIGHEST)
        return jnp.einsum('jkr,jr->kr', inner, factor_b, precision=HIGHEST)
    mttkrp_c = lax.map(third_mode, jnp.arange(N_COL, dtype=jnp.int32)).reshape(DIM_K, RANK)
    factor_c = normalize(solve_rows(mttkrp_c, gram_a, gram_b_new), DIM_K)
    return (factor_a, factor_b, factor_c)
```

```python
import jax
import jax.numpy as jnp
from jax import lax
from jax.sharding import Mesh, PartitionSpec as P

EPSILON = 1e-06
HIGHEST = lax.Precision.HIGHEST
F32 = jnp.float32


def dot(left, right):
    return jnp.dot(left, right, precision=HIGHEST, preferred_element_type=F32)


def gram_of(rows):
    return lax.dot_general(rows, rows, (((0,), (0,)), ((), ())), precision=HIGHEST, preferred_element_type=F32)


def spd_inverse(matrix):
    lower = jnp.linalg.cholesky(matrix)
    return jax.scipy.linalg.cho_solve((lower, True), jnp.eye(matrix.shape[0], dtype=F32))


def axes_size(axes):
    size = 1
    for axis in axes:
        size *= lax.axis_size(axis)
    return size


def gather(rows, axes):
    size = axes_size(axes)
    copies = jnp.broadcast_to(rows[None], (size,) + rows.shape)
    out = lax.all_to_all(copies, axes, 0, 0, tiled=True)
    return out.reshape((size * rows.shape[0],) + rows.shape[1:])


def reduce_scatter(partial, axes):
    size = axes_size(axes)
    parts = partial.reshape((size, partial.shape[0] // size) + partial.shape[1:])
    return jnp.sum(lax.all_to_all(parts, axes, 0, 0, tiled=True), axis=0)


def normalized(gram, total_rows):
    squares = jnp.sum(jnp.where(jnp.eye(gram.shape[0], dtype=bool), gram, 0.0), axis=0)
    inv_scale = 1.0 / jnp.sqrt(squares / total_rows + EPSILON)
    return inv_scale, gram * inv_scale[:, None] * inv_scale[None, :]


def body(tensor, b_row, c_row):
    blk_i, blk_j, blk_k = tensor.shape
    rank = b_row.shape[1]
    n_aa, n_y, n_core, n_col = (lax.axis_size(axis) for axis in ("aa", "y", "core", "col"))
    dim_i, dim_j, dim_k = blk_i * n_aa, blk_j * n_y * n_core, blk_k * n_col
    y, core, col = lax.axis_index("y"), lax.axis_index("core"), lax.axis_index("col")

    own = gather(jnp.concatenate([b_row, c_row], axis=1), ("aa", "y", "col"))
    other = lax.ppermute(own, "core", [(0, 1), (1, 0)])
    both = jnp.stack([jnp.where(core == 0, own, other), jnp.where(core == 0, other, own)])
    b_block = lax.dynamic_index_in_dim(
        own[:, :rank].reshape(n_aa, n_y, n_col, rank), y, 1, keepdims=False
    ).reshape(blk_j, rank)
    c_block = lax.dynamic_index_in_dim(
        both[:, :, rank:].astype(jnp.bfloat16).reshape(n_core, n_aa, n_y, n_col, rank), col, 3, keepdims=False
    )
    c_block = c_block.transpose(1, 2, 0, 3).reshape(blk_k, rank)
    gram_b = gram_of(both[:, :, :rank].reshape(dim_j, rank))
    gram_c = gram_of(both[:, :, rank:].reshape(dim_k, rank))

    inner = jnp.einsum("ijk,kr->ijr", tensor, c_block, preferred_element_type=F32)
    mttkrp_a = reduce_scatter(jnp.sum(inner * b_block[None], axis=1), ("y", "core", "col"))
    inverse = spd_inverse(gram_b * gram_c)
    raw_a = dot(gather(mttkrp_a, ("y", "core", "col")), inverse)
    all_a = gather(raw_a, ("aa",))

    mttkrp_b = reduce_scatter(jnp.sum(inner * raw_a[:, None], axis=0), ("aa", "col"))
    inv_scale_a, gram_a = normalized(gram_of(all_a), dim_i)
    factor_a = raw_a * inv_scale_a
    inverse = spd_inverse(gram_a * gram_c)
    raw_b = dot(gather(mttkrp_b, ("aa", "col")) * inv_scale_a, inverse)
    all_b = gather(raw_b, ("y", "core"))

    inner = jnp.einsum("ijk,ir->jkr", tensor, factor_a.astype(jnp.bfloat16), preferred_element_type=F32)
    mttkrp_c = reduce_scatter(jnp.sum(inner * raw_b[:, None], axis=0), ("aa", "y", "core"))
    inv_scale_b, gram_b_new = normalized(gram_of(all_b), dim_j)
    factor_b = raw_b * inv_scale_b
    inverse = spd_inverse(gram_a * gram_b_new)
    raw_c = dot(mttkrp_c * inv_scale_b, inverse)
    squares = jnp.sum(gather(raw_c * raw_c, ("y", "core", "col")), axis=0, keepdims=True)
    squares = jnp.sum(gather(squares, ("aa",)), axis=0, keepdims=True)
    factor_c = raw_c / jnp.sqrt(squares / dim_k + EPSILON)

    a_index = (y * n_core + core) * n_col + col
    b_index = lax.axis_index("aa") * n_col + col
    return (
        lax.dynamic_slice_in_dim(factor_a, a_index, 1, 0),
        lax.dynamic_slice_in_dim(factor_b, b_index, 1, 0),
        factor_c,
    )


def solution(mesh):
    n_aa, n_ba, n_col = mesh.devices.shape
    fine = Mesh(mesh.devices.reshape(n_aa, n_ba // 2, 2, n_col), ("aa", "y", "core", "col"))
    a_spec = P(("aa", "y", "core", "col"), None)
    b_spec = P(("y", "core", "aa", "col"), None)
    c_spec = P(("col", "aa", "y", "core"), None)
    return jax.shard_map(
        body,
        mesh=fine,
        in_specs=(P("aa", ("y", "core"), "col"), b_spec, c_spec),
        out_specs=(a_spec, b_spec, c_spec),
        check_vma=False,
    )
```

```python
import jax
import jax.numpy as jnp
from jax import lax
from jax.experimental import pallas as pl
from jax.experimental.pallas import tpu as pltpu
from jax.sharding import Mesh, PartitionSpec as P

EPSILON = 1e-06
HIGHEST = lax.Precision.HIGHEST
F32 = jnp.float32


def dot(left, right):
    return jnp.dot(left, right, precision=HIGHEST, preferred_element_type=F32)


def gram_of(rows):
    return lax.dot_general(rows, rows, (((0,), (0,)), ((), ())), precision=HIGHEST, preferred_element_type=F32)


SUB = 8
PANEL = 128


def invert_tile(columns, row_id):
    for k in range(SUB):
        inv = 1.0 / columns[k][k : k + 1, :]
        factor = jnp.where(row_id == k, -1.0, columns[k])
        columns = [
            -factor * inv
            if j == k
            else jnp.where(row_id == k, 0.0, columns[j]) - factor * (columns[j][k : k + 1, :] * inv)
            for j in range(SUB)
        ]
    return columns


def invert_panel(matrix):
    size = matrix.shape[0]
    row_id = lax.broadcasted_iota(jnp.int32, (SUB, size), 0)
    col_id = lax.broadcasted_iota(jnp.int32, (SUB, size), 1)
    tiles = [matrix[lo : lo + SUB, :] for lo in range(0, size, SUB)]
    for q in range(size // SUB):
        lo = q * SUB
        columns = [jnp.broadcast_to(tiles[q][:, lo + j : lo + j + 1], (SUB, size)) for j in range(SUB)]
        columns = invert_tile(columns, row_id)
        inside = (col_id >= lo) & (col_id < lo + SUB)
        pivot = jnp.where(inside, jnp.where(col_id - lo == row_id, 1.0, 0.0), tiles[q])
        rows = columns[0] * pivot[0:1, :]
        for j in range(1, SUB):
            rows = rows + columns[j] * pivot[j : j + 1, :]
        updated = []
        for i, tile in enumerate(tiles):
            if i == q:
                updated.append(rows)
                continue
            total = jnp.where(inside, 0.0, tile)
            for j in range(SUB):
                total = total - tile[:, lo + j : lo + j + 1] * rows[j : j + 1, :]
            updated.append(total)
        tiles = updated
    return jnp.concatenate(tiles, axis=0)


def invert_into(source, out_ref):
    size = source.shape[0]
    col_id = lax.broadcasted_iota(jnp.int32, (1, size), 1)
    for lo in range(0, size, PANEL):
        matrix = source if lo == 0 else out_ref[...]
        panel = matrix[lo : lo + PANEL, :]
        inverse = invert_panel(panel[:, lo : lo + PANEL])
        rows = dot(inverse, panel)
        parts = [rows[:, :lo]] * (lo > 0) + [inverse] + [rows[:, lo + PANEL :]] * (lo + PANEL < size)
        rows = jnp.concatenate(parts, axis=1)
        inside = (col_id >= lo) & (col_id < lo + PANEL)
        out_ref[...] = jnp.where(inside, 0.0, matrix) - dot(matrix[:, lo : lo + PANEL], rows)
        out_ref[lo : lo + PANEL, :] = rows


def given_kernel(own_ref, other_ref, inverse_ref, gram_c_ref):
    rank = inverse_ref.shape[0]
    gram_b = gram_of(own_ref[:, :rank]) + gram_of(other_ref[:, :rank])
    gram_c = gram_of(own_ref[:, rank:]) + gram_of(other_ref[:, rank:])
    gram_c_ref[...] = gram_c
    invert_into(gram_b * gram_c, inverse_ref)


def scaled_kernel(rows_ref, other_gram_ref, inverse_ref, gram_ref, inv_scale_ref):
    gram = gram_of(rows_ref[...])
    size = gram.shape[0]
    row_id = lax.broadcasted_iota(jnp.int32, (size, size), 0)
    col_id = lax.broadcasted_iota(jnp.int32, (size, size), 1)
    squares = jnp.where(row_id == col_id, gram, 0.0)
    by_col = 1.0 / jnp.sqrt(jnp.sum(squares, axis=0, keepdims=True) / rows_ref.shape[0] + EPSILON)
    by_row = 1.0 / jnp.sqrt(jnp.sum(squares, axis=1, keepdims=True) / rows_ref.shape[0] + EPSILON)
    gram = gram * by_row * by_col
    inv_scale_ref[...] = by_col
    gram_ref[...] = gram
    invert_into(gram * other_gram_ref[...], inverse_ref)


def local_call(kernel, out_shapes, *operands):
    vmem = pl.BlockSpec(memory_space=pltpu.VMEM)
    return pl.pallas_call(
        kernel,
        out_shape=[jax.ShapeDtypeStruct(shape, F32) for shape in out_shapes],
        in_specs=[vmem] * len(operands),
        out_specs=[vmem] * len(out_shapes),
        compiler_params=pltpu.CompilerParams(vmem_limit_bytes=24 * 2**20),
        cost_estimate=pl.CostEstimate(flops=6 * 2 * 10**9, bytes_accessed=2**21, transcendentals=0),
    )(*operands)


def axes_size(axes):
    size = 1
    for axis in axes:
        size *= lax.axis_size(axis)
    return size


def gather(rows, axes):
    size = axes_size(axes)
    copies = jnp.broadcast_to(rows[None], (size,) + rows.shape)
    out = lax.all_to_all(copies, axes, 0, 0, tiled=True)
    return out.reshape((size * rows.shape[0],) + rows.shape[1:])


def reduce_scatter(partial, axes):
    size = axes_size(axes)
    parts = partial.reshape((size, partial.shape[0] // size) + partial.shape[1:])
    return jnp.sum(lax.all_to_all(parts, axes, 0, 0, tiled=True), axis=0)


def body(tensor, b_row, c_row):
    blk_i, blk_j, blk_k = tensor.shape
    rank = b_row.shape[1]
    n_aa, n_y, n_core, n_col = (lax.axis_size(axis) for axis in ("aa", "y", "core", "col"))
    dim_k = blk_k * n_col
    y, core, col = lax.axis_index("y"), lax.axis_index("core"), lax.axis_index("col")

    own = gather(jnp.concatenate([b_row, c_row], axis=1), ("aa", "y", "col"))
    other = lax.ppermute(own, "core", [(0, 1), (1, 0)])
    both = jnp.stack([jnp.where(core == 0, own, other), jnp.where(core == 0, other, own)])
    b_block = lax.dynamic_index_in_dim(
        own[:, :rank].reshape(n_aa, n_y, n_col, rank), y, 1, keepdims=False
    ).reshape(blk_j, rank)
    c_block = lax.dynamic_index_in_dim(
        both[:, :, rank:].astype(jnp.bfloat16).reshape(n_core, n_aa, n_y, n_col, rank), col, 3, keepdims=False
    )
    c_block = c_block.transpose(1, 2, 0, 3).reshape(blk_k, rank)

    inner = jnp.einsum("ijk,kr->ijr", tensor, c_block, preferred_element_type=F32)
    mttkrp_a = reduce_scatter(jnp.sum(inner * b_block[None], axis=1), ("y", "core", "col"))
    square = (rank, rank)
    inverse, gram_c = local_call(given_kernel, [square, square], own, other)
    raw_a = dot(gather(mttkrp_a, ("y", "core", "col")), inverse)
    all_a = gather(raw_a, ("aa",))

    mttkrp_b = reduce_scatter(jnp.sum(inner * raw_a[:, None], axis=0), ("aa", "col"))
    inverse, gram_a, inv_scale_a = local_call(scaled_kernel, [square, square, (1, rank)], all_a, gram_c)
    factor_a = raw_a * inv_scale_a
    raw_b = dot(gather(mttkrp_b, ("aa", "col")) * inv_scale_a, inverse)
    all_b = gather(raw_b, ("y", "core"))

    inner = jnp.einsum("ijk,ir->jkr", tensor, factor_a.astype(jnp.bfloat16), preferred_element_type=F32)
    mttkrp_c = reduce_scatter(jnp.sum(inner * raw_b[:, None], axis=0), ("aa", "y", "core"))
    inverse, _, inv_scale_b = local_call(scaled_kernel, [square, square, (1, rank)], all_b, gram_a)
    factor_b = raw_b * inv_scale_b
    raw_c = dot(mttkrp_c * inv_scale_b, inverse)
    squares = jnp.sum(gather(raw_c * raw_c, ("y", "core", "col")), axis=0, keepdims=True)
    squares = jnp.sum(gather(squares, ("aa",)), axis=0, keepdims=True)
    factor_c = raw_c / jnp.sqrt(squares / dim_k + EPSILON)

    a_index = (y * n_core + core) * n_col + col
    b_index = lax.axis_index("aa") * n_col + col
    return (
        lax.dynamic_slice_in_dim(factor_a, a_index, 1, 0),
        lax.dynamic_slice_in_dim(factor_b, b_index, 1, 0),
        factor_c,
    )


def solution(mesh):
    n_aa, n_ba, n_col = mesh.devices.shape
    fine = Mesh(mesh.devices.reshape(n_aa, n_ba // 2, 2, n_col), ("aa", "y", "core", "col"))
    a_spec = P(("aa", "y", "core", "col"), None)
    b_spec = P(("y", "core", "aa", "col"), None)
    c_spec = P(("col", "aa", "y", "core"), None)
    return jax.shard_map(
        body,
        mesh=fine,
        in_specs=(P("aa", ("y", "core"), "col"), b_spec, c_spec),
        out_specs=(a_spec, b_spec, c_spec),
        check_vma=False,
    )
```

```python
import jax
import jax.numpy as jnp
from jax import lax
from jax.experimental import pallas as pl
from jax.experimental.pallas import tpu as pltpu
from jax.sharding import Mesh, PartitionSpec as P

EPSILON = 1e-06
HIGHEST = lax.Precision.HIGHEST
F32 = jnp.float32


def dot(left, right):
    return jnp.dot(left, right, precision=HIGHEST, preferred_element_type=F32)


def gram_of(rows):
    return lax.dot_general(rows, rows, (((0,), (0,)), ((), ())), precision=HIGHEST, preferred_element_type=F32)


SUB = 8
PANEL = 128


def invert_tile(columns, row_id):
    for k in range(SUB):
        inv = 1.0 / columns[k][k : k + 1, :]
        factor = jnp.where(row_id == k, -1.0, columns[k])
        columns = [
            -factor * inv
            if j == k
            else jnp.where(row_id == k, 0.0, columns[j]) - factor * (columns[j][k : k + 1, :] * inv)
            for j in range(SUB)
        ]
    return columns


def invert_panel(matrix):
    size = matrix.shape[0]
    row_id = lax.broadcasted_iota(jnp.int32, (SUB, size), 0)
    col_id = lax.broadcasted_iota(jnp.int32, (SUB, size), 1)
    tiles = [matrix[lo : lo + SUB, :] for lo in range(0, size, SUB)]
    for q in range(size // SUB):
        lo = q * SUB
        columns = [jnp.broadcast_to(tiles[q][:, lo + j : lo + j + 1], (SUB, size)) for j in range(SUB)]
        columns = invert_tile(columns, row_id)
        inside = (col_id >= lo) & (col_id < lo + SUB)
        pivot = jnp.where(inside, jnp.where(col_id - lo == row_id, 1.0, 0.0), tiles[q])
        rows = columns[0] * pivot[0:1, :]
        for j in range(1, SUB):
            rows = rows + columns[j] * pivot[j : j + 1, :]
        updated = []
        for i, tile in enumerate(tiles):
            if i == q:
                updated.append(rows)
                continue
            total = jnp.where(inside, 0.0, tile)
            for j in range(SUB):
                total = total - tile[:, lo + j : lo + j + 1] * rows[j : j + 1, :]
            updated.append(total)
        tiles = updated
    return jnp.concatenate(tiles, axis=0)


def invert_into(source, out_ref):
    size = source.shape[0]
    col_id = lax.broadcasted_iota(jnp.int32, (1, size), 1)
    for lo in range(0, size, PANEL):
        matrix = source if lo == 0 else out_ref[...]
        panel = matrix[lo : lo + PANEL, :]
        inverse = invert_panel(panel[:, lo : lo + PANEL])
        rows = dot(inverse, panel)
        parts = [rows[:, :lo]] * (lo > 0) + [inverse] + [rows[:, lo + PANEL :]] * (lo + PANEL < size)
        rows = jnp.concatenate(parts, axis=1)
        inside = (col_id >= lo) & (col_id < lo + PANEL)
        out_ref[...] = jnp.where(inside, 0.0, matrix) - dot(matrix[:, lo : lo + PANEL], rows)
        out_ref[lo : lo + PANEL, :] = rows


def given_kernel(own_ref, other_ref, inverse_ref, gram_c_ref):
    rank = inverse_ref.shape[0]
    gram_b = gram_of(own_ref[:, :rank]) + gram_of(other_ref[:, :rank])
    gram_c = gram_of(own_ref[:, rank:]) + gram_of(other_ref[:, rank:])
    gram_c_ref[...] = gram_c
    invert_into(gram_b * gram_c, inverse_ref)


def scaled_kernel(own_ref, other_ref, solve_ref, other_gram_ref, next_ref, gram_ref, inv_scale_ref):
    gram = gram_of(dot(own_ref[...], solve_ref[...])) + gram_of(dot(other_ref[...], solve_ref[...]))
    size = gram.shape[0]
    total_rows = 2 * own_ref.shape[0]
    row_id = lax.broadcasted_iota(jnp.int32, (size, size), 0)
    col_id = lax.broadcasted_iota(jnp.int32, (size, size), 1)
    squares = jnp.where(row_id == col_id, gram, 0.0)
    by_col = 1.0 / jnp.sqrt(jnp.sum(squares, axis=0, keepdims=True) / total_rows + EPSILON)
    by_row = 1.0 / jnp.sqrt(jnp.sum(squares, axis=1, keepdims=True) / total_rows + EPSILON)
    gram = gram * by_row * by_col
    inv_scale_ref[...] = by_col
    gram_ref[...] = gram
    invert_into(gram * other_gram_ref[...], next_ref)
    next_ref[...] = next_ref[...] * by_row


def local_call(kernel, out_shapes, *operands):
    vmem = pl.BlockSpec(memory_space=pltpu.VMEM)
    return pl.pallas_call(
        kernel,
        out_shape=[jax.ShapeDtypeStruct(shape, F32) for shape in out_shapes],
        in_specs=[vmem] * len(operands),
        out_specs=[vmem] * len(out_shapes),
        compiler_params=pltpu.CompilerParams(vmem_limit_bytes=24 * 2**20),
        cost_estimate=pl.CostEstimate(flops=6 * 2 * 10**9, bytes_accessed=2**21, transcendentals=0),
    )(*operands)


def axes_size(axes):
    size = 1
    for axis in axes:
        size *= lax.axis_size(axis)
    return size


def gather(rows, axes):
    size = axes_size(axes)
    copies = jnp.broadcast_to(rows[None], (size,) + rows.shape)
    out = lax.all_to_all(copies, axes, 0, 0, tiled=True)
    return out.reshape((size * rows.shape[0],) + rows.shape[1:])


def reduce_scatter(partial, axes):
    size = axes_size(axes)
    parts = partial.reshape((size, partial.shape[0] // size) + partial.shape[1:])
    return jnp.sum(lax.all_to_all(parts, axes, 0, 0, tiled=True), axis=0)


def gather_all(rows):
    own = gather(rows, ("aa", "y", "col"))
    return own, lax.ppermute(own, "core", [(0, 1), (1, 0)])


def body(tensor, b_row, c_row):
    blk_i, blk_j, blk_k = tensor.shape
    rank = b_row.shape[1]
    n_aa, n_y, n_core, n_col = (lax.axis_size(axis) for axis in ("aa", "y", "core", "col"))
    aa, y, core, col = (lax.axis_index(axis) for axis in ("aa", "y", "core", "col"))
    square = (rank, rank)

    def pick(rows, axis, index):
        return lax.dynamic_index_in_dim(rows.reshape(n_aa, n_y, n_col, rows.shape[1]), index, axis, keepdims=False)

    def by_core(own, other):
        return jnp.where(core == 0, own, other), jnp.where(core == 0, other, own)

    own, other = gather_all(jnp.concatenate([b_row, c_row], axis=1))
    b_block = pick(own, 1, y)[:, :, :rank].reshape(blk_j, rank)
    pair = by_core(pick(own, 2, col)[:, :, rank:], pick(other, 2, col)[:, :, rank:])
    c_block = jnp.stack(pair, axis=2).reshape(blk_k, rank).astype(jnp.bfloat16)

    inner = jnp.einsum("ijk,kr->ijr", tensor, c_block, preferred_element_type=F32)
    row = reduce_scatter(jnp.sum(inner * b_block[None], axis=1), ("y", "core", "col"))
    solve, gram_c = local_call(given_kernel, [square, square], own, other)
    own, other = gather_all(row)
    pair = by_core(pick(own, 0, aa), pick(other, 0, aa))
    raw_a = dot(jnp.stack(pair, axis=1).reshape(blk_i, rank), solve)

    row = reduce_scatter(jnp.sum(inner * raw_a[:, None], axis=0), ("aa", "col"))
    solve, gram_a, inv_scale_a = local_call(
        scaled_kernel, [square, square, (1, rank)], own, other, solve, gram_c
    )
    factor_a = raw_a * inv_scale_a
    own, other = gather_all(row)
    raw_b = dot(pick(own, 1, y).reshape(blk_j, rank), solve)

    inner = jnp.einsum("ijk,ir->jkr", tensor, factor_a.astype(jnp.bfloat16), preferred_element_type=F32)
    row = reduce_scatter(jnp.sum(inner * raw_b[:, None], axis=0), ("aa", "y", "core"))
    solve, _, inv_scale_b = local_call(
        scaled_kernel, [square, square, (1, rank)], own, other, solve, gram_a
    )
    factor_a = lax.dynamic_slice_in_dim(factor_a, (y * n_core + core) * n_col + col, 1, 0)
    factor_b = lax.dynamic_slice_in_dim(raw_b, aa * n_col + col, 1, 0) * inv_scale_b
    row, factor_a, factor_b = lax.optimization_barrier((row, factor_a, factor_b))

    raw_c = dot(row, solve)
    squares = jnp.sum(gather(raw_c * raw_c, ("aa", "core")), axis=0, keepdims=True)
    squares = jnp.sum(gather(squares, ("y", "col")), axis=0, keepdims=True)
    factor_c = raw_c / jnp.sqrt(squares / (blk_k * n_col) + EPSILON)
    return factor_a, factor_b, factor_c


def solution(mesh):
    n_aa, n_ba, n_col = mesh.devices.shape
    fine = Mesh(mesh.devices.reshape(n_aa, n_ba // 2, 2, n_col), ("aa", "y", "core", "col"))
    a_spec = P(("aa", "y", "core", "col"), None)
    b_spec = P(("y", "core", "aa", "col"), None)
    c_spec = P(("col", "aa", "y", "core"), None)
    return jax.shard_map(
        body,
        mesh=fine,
        in_specs=(P("aa", ("y", "core"), "col"), b_spec, c_spec),
        out_specs=(a_spec, b_spec, c_spec),
        check_vma=False,
    )
```

```python
import functools

import jax
import jax.numpy as jnp
from jax import lax
from jax.experimental import pallas as pl
from jax.experimental.pallas import tpu as pltpu
from jax.sharding import Mesh, PartitionSpec as P

EPSILON = 1e-06
HIGHEST = lax.Precision.HIGHEST
F32 = jnp.float32


def dot(left, right):
    return jnp.dot(left, right, precision=HIGHEST, preferred_element_type=F32)


def gram_of(rows):
    return lax.dot_general(rows, rows, (((0,), (0,)), ((), ())), precision=HIGHEST, preferred_element_type=F32)


SUB = 8
PANEL = 128


def invert_tile(columns, row_id):
    for k in range(SUB):
        inv = 1.0 / columns[k][k : k + 1, :]
        factor = jnp.where(row_id == k, -1.0, columns[k])
        columns = [
            -factor * inv
            if j == k
            else jnp.where(row_id == k, 0.0, columns[j]) - factor * (columns[j][k : k + 1, :] * inv)
            for j in range(SUB)
        ]
    return columns


def invert_panel(matrix):
    size = matrix.shape[0]
    row_id = lax.broadcasted_iota(jnp.int32, (SUB, size), 0)
    col_id = lax.broadcasted_iota(jnp.int32, (SUB, size), 1)
    tiles = [matrix[lo : lo + SUB, :] for lo in range(0, size, SUB)]
    for q in range(size // SUB):
        lo = q * SUB
        columns = [jnp.broadcast_to(tiles[q][:, lo + j : lo + j + 1], (SUB, size)) for j in range(SUB)]
        columns = invert_tile(columns, row_id)
        inside = (col_id >= lo) & (col_id < lo + SUB)
        pivot = jnp.where(inside, jnp.where(col_id - lo == row_id, 1.0, 0.0), tiles[q])
        rows = columns[0] * pivot[0:1, :]
        for j in range(1, SUB):
            rows = rows + columns[j] * pivot[j : j + 1, :]
        updated = []
        for i, tile in enumerate(tiles):
            if i == q:
                updated.append(rows)
                continue
            total = jnp.where(inside, 0.0, tile)
            for j in range(SUB):
                total = total - tile[:, lo + j : lo + j + 1] * rows[j : j + 1, :]
            updated.append(total)
        tiles = updated
    return jnp.concatenate(tiles, axis=0)


def invert_into(source, out_ref):
    size = source.shape[0]
    col_id = lax.broadcasted_iota(jnp.int32, (1, size), 1)
    for lo in range(0, size, PANEL):
        matrix = source if lo == 0 else out_ref[...]
        panel = matrix[lo : lo + PANEL, :]
        inverse = invert_panel(panel[:, lo : lo + PANEL])
        rows = dot(inverse, panel)
        parts = [rows[:, :lo]] * (lo > 0) + [inverse] + [rows[:, lo + PANEL :]] * (lo + PANEL < size)
        rows = jnp.concatenate(parts, axis=1)
        inside = (col_id >= lo) & (col_id < lo + PANEL)
        out_ref[...] = jnp.where(inside, 0.0, matrix) - dot(matrix[:, lo : lo + PANEL], rows)
        out_ref[lo : lo + PANEL, :] = rows


def given_kernel(own_ref, other_ref, _, inverse_ref, gram_c_ref):
    rank = inverse_ref.shape[0]
    gram_b = gram_of(own_ref[:, :rank]) + gram_of(other_ref[:, :rank])
    gram_c = gram_of(own_ref[:, rank:]) + gram_of(other_ref[:, rank:])
    gram_c_ref[...] = gram_c
    invert_into(gram_b * gram_c, inverse_ref)


def scaled_kernel(own_ref, other_ref, solve_ref, other_gram_ref, raw_ref, _, next_ref, gram_ref, inv_scale_ref, row_ref):
    gram = gram_of(dot(own_ref[...], solve_ref[...])) + gram_of(dot(other_ref[...], solve_ref[...]))
    size = gram.shape[0]
    total_rows = 2 * own_ref.shape[0]
    row_id = lax.broadcasted_iota(jnp.int32, (size, size), 0)
    col_id = lax.broadcasted_iota(jnp.int32, (size, size), 1)
    squares = jnp.where(row_id == col_id, gram, 0.0)
    by_col = 1.0 / jnp.sqrt(jnp.sum(squares, axis=0, keepdims=True) / total_rows + EPSILON)
    by_row = 1.0 / jnp.sqrt(jnp.sum(squares, axis=1, keepdims=True) / total_rows + EPSILON)
    gram = gram * by_row * by_col
    inv_scale_ref[...] = by_col
    row_ref[...] = raw_ref[...] * by_col
    gram_ref[...] = gram
    invert_into(gram * other_gram_ref[...], next_ref)
    next_ref[...] = next_ref[...] * by_row


def spread_kernel(parts_ref, *refs):
    out_ref = refs[-1]
    total = jnp.sum(parts_ref[...], axis=0)
    out_ref[...] = jnp.broadcast_to(total[None], out_ref.shape)


def apply_kernel(parts_ref, solve_ref, raw_ref, squares_ref):
    raw = dot(jnp.sum(parts_ref[...], axis=0), solve_ref[...])
    raw_ref[...] = raw
    squares_ref[...] = jnp.broadcast_to((raw * raw)[None], squares_ref.shape)


def scale_kernel(total_rows, parts_ref, raw_ref, out_ref):
    squares = jnp.sum(parts_ref[...], axis=0)
    out_ref[...] = raw_ref[...] / jnp.sqrt(squares / total_rows + EPSILON)


def local_call(kernel, out_shapes, *operands, flops=10**6, waits=0):
    vmem = pl.BlockSpec(memory_space=pltpu.VMEM)
    kept = pl.BlockSpec(memory_space=pl.ANY)
    return pl.pallas_call(
        kernel,
        out_shape=[jax.ShapeDtypeStruct(shape, F32) for shape in out_shapes],
        in_specs=[vmem] * (len(operands) - waits) + [kept] * waits,
        out_specs=[vmem] * len(out_shapes),
        compiler_params=pltpu.CompilerParams(vmem_limit_bytes=24 * 2**20),
        cost_estimate=pl.CostEstimate(flops=flops, bytes_accessed=2**20, transcendentals=0),
    )(*operands)


def axes_size(axes):
    size = 1
    for axis in axes:
        size *= lax.axis_size(axis)
    return size


def exchange(blocks, axes):
    return lax.all_to_all(blocks, axes, 0, 0, tiled=True)


def split(partial, axes):
    size = axes_size(axes)
    return exchange(partial.reshape(size, partial.shape[0] // size, partial.shape[1]), axes)


PLANE = ("aa", "y", "col")


def gather_all(copies):
    own = exchange(copies, PLANE).reshape(copies.shape[0], copies.shape[2])
    return own, lax.ppermute(own, "core", [(0, 1), (1, 0)])


def body(tensor, b_row, c_row):
    blk_i, blk_j, blk_k = tensor.shape
    rank = b_row.shape[1]
    n_aa, n_y, n_core, n_col = (lax.axis_size(axis) for axis in ("aa", "y", "core", "col"))
    aa, y, core, col = (lax.axis_index(axis) for axis in ("aa", "y", "core", "col"))
    square, heavy = (rank, rank), 12 * 10**9

    def pick(rows, axis, index):
        return lax.dynamic_index_in_dim(rows.reshape(n_aa, n_y, n_col, rows.shape[1]), index, axis, keepdims=False)

    def by_core(own, other):
        return jnp.where(core == 0, own, other), jnp.where(core == 0, other, own)

    planes = axes_size(PLANE)
    copies = (planes, 1, rank)
    given = jnp.concatenate([b_row, c_row], axis=1)[None]
    own, other = gather_all(jnp.broadcast_to(given, (planes, 1, 2 * rank)))
    b_block = pick(own, 1, y)[:, :, :rank].reshape(blk_j, rank)
    pair = by_core(pick(own, 2, col)[:, :, rank:], pick(other, 2, col)[:, :, rank:])
    c_block = jnp.stack(pair, axis=2).reshape(blk_k, rank).astype(jnp.bfloat16)

    inner = jnp.einsum("ijk,kr->ijr", tensor, c_block, preferred_element_type=F32)
    partial = jnp.sum(inner * b_block[None], axis=1)
    parts = split(partial, ("y", "core", "col"))
    solve, gram_c = local_call(given_kernel, [square, square], own, other, partial, flops=heavy, waits=1)
    own, other = gather_all(local_call(spread_kernel, [copies], parts, solve, waits=1)[0])
    pair = by_core(pick(own, 0, aa), pick(other, 0, aa))
    raw_a = dot(jnp.stack(pair, axis=1).reshape(blk_i, rank), solve)

    partial = jnp.sum(inner * raw_a[:, None], axis=0)
    parts = split(partial, ("aa", "col"))
    row = lax.dynamic_slice_in_dim(raw_a, (y * n_core + core) * n_col + col, 1, 0)
    solve, gram_a, inv_scale_a, factor_a = local_call(
        scaled_kernel,
        [square, square, (1, rank), (1, rank)],
        own, other, solve, gram_c, row, partial,
        flops=heavy, waits=1,
    )
    a_low = (raw_a * inv_scale_a).astype(jnp.bfloat16)
    own, other = gather_all(local_call(spread_kernel, [copies], parts, solve, waits=1)[0])
    raw_b = dot(pick(own, 1, y).reshape(blk_j, rank), solve)

    inner = jnp.einsum("ijk,ir->jkr", tensor, a_low, preferred_element_type=F32)
    partial = jnp.sum(inner * raw_b[:, None], axis=0)
    parts = split(partial, ("aa", "y", "core"))
    row = lax.dynamic_slice_in_dim(raw_b, aa * n_col + col, 1, 0)
    solve, _, _, factor_b = local_call(
        scaled_kernel,
        [square, square, (1, rank), (1, rank)],
        own, other, solve, gram_a, row, partial,
        flops=heavy, waits=1,
    )

    near, far = ("aa", "core"), ("y", "col")
    raw_c, squares = local_call(apply_kernel, [(1, rank), (axes_size(near), 1, rank)], parts, solve)
    squares = local_call(spread_kernel, [(axes_size(far), 1, rank)], exchange(squares, near))[0]
    scale = functools.partial(scale_kernel, blk_k * n_col)
    factor_c = local_call(scale, [(1, rank)], exchange(squares, far), raw_c)[0]
    return factor_a, factor_b, factor_c


def solution(mesh):
    n_aa, n_ba, n_col = mesh.devices.shape
    fine = Mesh(mesh.devices.reshape(n_aa, n_ba // 2, 2, n_col), ("aa", "y", "core", "col"))
    a_spec = P(("aa", "y", "core", "col"), None)
    b_spec = P(("y", "core", "aa", "col"), None)
    c_spec = P(("col", "aa", "y", "core"), None)
    return jax.shard_map(
        body,
        mesh=fine,
        in_specs=(P("aa", ("y", "core"), "col"), b_spec, c_spec),
        out_specs=(a_spec, b_spec, c_spec),
        check_vma=False,
    )
```

```python
import functools

import jax
import jax.numpy as jnp
from jax import lax
from jax.experimental import pallas as pl
from jax.experimental.pallas import tpu as pltpu
from jax.sharding import Mesh, PartitionSpec as P

EPSILON = 1e-06
HIGHEST = lax.Precision.HIGHEST
F32 = jnp.float32


def dot(left, right):
    return jnp.dot(left, right, precision=HIGHEST, preferred_element_type=F32)


def gram_of(rows):
    return lax.dot_general(rows, rows, (((0,), (0,)), ((), ())), precision=HIGHEST, preferred_element_type=F32)


SUB = 8
PANEL = 128
N_COL = 4


def tree_sum(terms):
    while len(terms) > 1:
        terms = [terms[n] + terms[n + 1] if n + 1 < len(terms) else terms[n] for n in range(0, len(terms), 2)]
    return terms[0]


def invert_tile(columns, row_id):
    for k in range(0, SUB, 2):
        a, b = columns[k][k : k + 1, :], columns[k + 1][k : k + 1, :]
        c, d = columns[k][k + 1 : k + 2, :], columns[k + 1][k + 1 : k + 2, :]
        inv = 1.0 / (a * d - b * c)
        first = (d * inv, -b * inv)
        second = (-c * inv, a * inv)
        inside = (row_id == k) | (row_id == k + 1)
        left = jnp.where(row_id == k, -1.0, jnp.where(row_id == k + 1, 0.0, columns[k]))
        right = jnp.where(row_id == k + 1, -1.0, jnp.where(row_id == k, 0.0, columns[k + 1]))
        updated = []
        for j in range(SUB):
            if j in (k, k + 1):
                top, low, base = first[j - k], second[j - k], 0.0
            else:
                x, y = columns[j][k : k + 1, :], columns[j][k + 1 : k + 2, :]
                top, low = first[0] * x + first[1] * y, second[0] * x + second[1] * y
                base = jnp.where(inside, 0.0, columns[j])
            updated.append(base - (left * top + right * low))
        columns = updated
    return columns


def invert_panel(matrix):
    size = matrix.shape[0]
    row_id = lax.broadcasted_iota(jnp.int32, (SUB, size), 0)
    col_id = lax.broadcasted_iota(jnp.int32, (SUB, size), 1)
    tiles = [matrix[lo : lo + SUB, :] for lo in range(0, size, SUB)]
    plain, scaled = [], []
    for q in range(size // SUB):
        lo = q * SUB
        columns = [jnp.broadcast_to(tiles[q][:, lo + j : lo + j + 1], (SUB, size)) for j in range(SUB)]
        columns = invert_tile(columns, row_id)
        inside = (col_id >= lo) & (col_id < lo + SUB)
        pivot = jnp.where(inside, jnp.where(col_id - lo == row_id, 1.0, 0.0), tiles[q])
        rows = tree_sum([columns[j] * pivot[j : j + 1, :] for j in range(SUB)])
        known = col_id < lo + SUB
        plain.append(jnp.where(known, pivot, 0.0))
        scaled.append(jnp.where(known, rows, 0.0))
        for i in range(q + 1, size // SUB):
            tile = tiles[i]
            terms = [tile[:, lo + j : lo + j + 1] * rows[j : j + 1, :] for j in range(SUB)]
            tiles[i] = jnp.where(inside, 0.0, tile) - tree_sum(terms)
    return lax.dot_general(
        jnp.concatenate(plain, axis=0),
        jnp.concatenate(scaled, axis=0),
        (((0,), (0,)), ((), ())),
        precision=HIGHEST,
        preferred_element_type=F32,
    )


def invert_into(matrix, out_ref):
    head = matrix[:PANEL, :PANEL]
    cross = matrix[:PANEL, PANEL:]
    head_inverse = invert_panel(head)
    solved = dot(head_inverse, cross)
    tail_inverse = invert_panel(matrix[PANEL:, PANEL:] - dot(matrix[PANEL:, :PANEL], solved))
    mixed = dot(solved, tail_inverse)
    out_ref[PANEL:, PANEL:] = tail_inverse
    out_ref[:PANEL, PANEL:] = -mixed
    out_ref[PANEL:, :PANEL] = -mixed.T
    out_ref[:PANEL, :PANEL] = head_inverse + lax.dot_general(
        mixed, solved, (((1,), (1,)), ((), ())), precision=HIGHEST, preferred_element_type=F32
    )


ROWS = 8


def one_hot(shape, wanted):
    return jnp.where(lax.broadcasted_iota(jnp.int32, shape, 1) == wanted, 1.0, 0.0)


def first_kernel(place_ref, tensor_ref, own_ref, other_ref, c_block_ref, out_ref):
    y, core, col = place_ref[1], place_ref[2], place_ref[3]
    blk_i, blk_j, blk_k = tensor_ref.shape
    plane, rank = own_ref.shape[0], c_block_ref.shape[1]
    n_col = N_COL
    k = lax.broadcasted_iota(jnp.int32, (blk_k, plane), 0)
    at = k // 16 * (8 * n_col) + k % 16 // 2 * n_col + col
    c_low_own = own_ref[:, rank:].astype(jnp.bfloat16)
    c_low_other = other_ref[:, rank:].astype(jnp.bfloat16)
    mine = k % 2 == core
    pick_own = one_hot((blk_k, plane), jnp.where(mine, at, -1)).astype(jnp.bfloat16)
    pick_other = one_hot((blk_k, plane), jnp.where(mine, -1, at)).astype(jnp.bfloat16)
    c_block = jnp.dot(pick_own, c_low_own, preferred_element_type=F32) + jnp.dot(
        pick_other, c_low_other, preferred_element_type=F32
    )
    c_block = c_block.astype(jnp.bfloat16)
    c_block_ref[...] = c_block
    j = lax.broadcasted_iota(jnp.int32, (blk_j, plane), 0)
    b_block = dot(one_hot((blk_j, plane), j // n_col * (8 * n_col) + y * n_col + j % n_col), own_ref[:, :rank])
    for lo in range(0, blk_i, ROWS):
        flat = tensor_ref[lo : lo + ROWS].reshape(ROWS * blk_j, blk_k)
        inner = jnp.dot(flat, c_block, preferred_element_type=F32)
        for i in range(lo, lo + ROWS):
            row = jnp.sum(inner[(i - lo) * blk_j : (i - lo + 1) * blk_j] * b_block, axis=0, keepdims=True)
            for copy in range(n_col):
                out_ref[i // n_col * n_col + copy, i % n_col : i % n_col + 1, :] = row


def second_kernel(place_ref, tensor_ref, c_block_ref, own_ref, other_ref, solve_ref, raw_ref, row_ref, out_ref):
    aa, y, core, col = place_ref[0], place_ref[1], place_ref[2], place_ref[3]
    blk_i, blk_j, blk_k = tensor_ref.shape
    half = blk_i // 2
    n_col = N_COL
    lo = pl.multiple_of(aa * half, half)
    raw_own = dot(own_ref[pl.ds(lo, half), :], solve_ref[...])
    raw_other = dot(other_ref[pl.ds(lo, half), :], solve_ref[...])
    even = jnp.where(core == 0, raw_own, raw_other)
    odd = jnp.where(core == 0, raw_other, raw_own)
    for step in range(half // n_col):
        raw_ref[2 * step * n_col : (2 * step + 1) * n_col, :] = even[step * n_col : (step + 1) * n_col]
        raw_ref[(2 * step + 1) * n_col : (2 * step + 2) * n_col, :] = odd[step * n_col : (step + 1) * n_col]
    row_ref[...] = raw_ref[pl.ds((2 * y + core) * n_col + col, 1), :]
    c_block = c_block_ref[...]
    total = jnp.zeros((blk_j, row_ref.shape[1]), F32)
    for lo in range(0, blk_i, ROWS):
        flat = tensor_ref[lo : lo + ROWS].reshape(ROWS * blk_j, blk_k)
        inner = jnp.dot(flat, c_block, preferred_element_type=F32)
        for i in range(ROWS):
            total = total + inner[i * blk_j : (i + 1) * blk_j] * raw_ref[lo + i : lo + i + 1, :]
    rows = out_ref.shape[1]
    for dest in range(out_ref.shape[0]):
        lo = dest % n_col * blk_j // n_col // rows * rows
        out_ref[dest] = total[lo : lo + rows]


def given_kernel(own_ref, other_ref, _, inverse_ref, gram_c_ref):
    rank = inverse_ref.shape[0]
    gram_b = gram_of(own_ref[:, :rank]) + gram_of(other_ref[:, :rank])
    gram_c = gram_of(own_ref[:, rank:]) + gram_of(other_ref[:, rank:])
    gram_c_ref[...] = gram_c
    invert_into(gram_b * gram_c, inverse_ref)


def scaled_kernel(
    own_ref, other_ref, solve_ref, other_gram_ref, block_ref, row_ref, _, next_ref, gram_ref, low_ref, out_row_ref
):
    gram = gram_of(dot(own_ref[...], solve_ref[...])) + gram_of(dot(other_ref[...], solve_ref[...]))
    size = gram.shape[0]
    total_rows = 2 * own_ref.shape[0]
    row_id = lax.broadcasted_iota(jnp.int32, (size, size), 0)
    col_id = lax.broadcasted_iota(jnp.int32, (size, size), 1)
    squares = jnp.where(row_id == col_id, gram, 0.0)
    by_col = 1.0 / jnp.sqrt(jnp.sum(squares, axis=0, keepdims=True) / total_rows + EPSILON)
    by_row = 1.0 / jnp.sqrt(jnp.sum(squares, axis=1, keepdims=True) / total_rows + EPSILON)
    gram = gram * by_row * by_col
    low_ref[...] = (block_ref[...] * by_col).astype(low_ref.dtype)
    out_row_ref[...] = row_ref[...] * by_col
    gram_ref[...] = gram
    invert_into(gram * other_gram_ref[...], next_ref)
    next_ref[...] = next_ref[...] * by_row


def given_copies_kernel(b_ref, c_ref, out_ref):
    row = jnp.concatenate([b_ref[...], c_ref[...]], axis=1)
    out_ref[...] = jnp.broadcast_to(row[None], out_ref.shape)


def spread_kernel(parts_ref, *refs):
    out_ref = refs[-1]
    total = jnp.sum(parts_ref[...], axis=0)
    out_ref[...] = jnp.broadcast_to(total[None], out_ref.shape)


def apply_kernel(parts_ref, solve_ref, raw_ref, squares_ref):
    raw = dot(jnp.sum(parts_ref[...], axis=0), solve_ref[...])
    raw_ref[...] = raw
    squares_ref[...] = jnp.broadcast_to((raw * raw)[None], squares_ref.shape)


def scale_kernel(total_rows, parts_ref, raw_ref, out_ref):
    squares = jnp.sum(parts_ref[...], axis=0)
    out_ref[...] = raw_ref[...] / jnp.sqrt(squares / total_rows + EPSILON)


def local_call(kernel, out_shapes, *operands, flops=10**6, waits=0, place=None):
    vmem = pl.BlockSpec(memory_space=pltpu.VMEM)
    specs = [vmem] * (len(operands) - waits) + [pl.BlockSpec(memory_space=pl.ANY)] * waits
    if place is not None:
        operands, specs = (place,) + operands, [pl.BlockSpec(memory_space=pltpu.SMEM)] + specs
    return pl.pallas_call(
        kernel,
        out_shape=[s if isinstance(s, jax.ShapeDtypeStruct) else jax.ShapeDtypeStruct(s, F32) for s in out_shapes],
        in_specs=specs,
        out_specs=[vmem] * len(out_shapes),
        compiler_params=pltpu.CompilerParams(vmem_limit_bytes=24 * 2**20),
        cost_estimate=pl.CostEstimate(flops=flops, bytes_accessed=2**20, transcendentals=0),
    )(*operands)


def axes_size(axes):
    size = 1
    for axis in axes:
        size *= lax.axis_size(axis)
    return size


def exchange(blocks, axes):
    return lax.all_to_all(blocks, axes, 0, 0, tiled=True)


COL = ("col_hi", "col_lo")
PLANE = ("aa", "y") + COL


def gather_all(copies, axes):
    own = exchange(copies, axes).reshape(copies.shape[0] * copies.shape[1], copies.shape[2])
    return own, lax.ppermute(own, "core", [(0, 1), (1, 0)])


def body(tensor, b_row, c_row):
    blk_i, blk_j, blk_k = tensor.shape
    rank = b_row.shape[1]
    n_aa, n_y, n_core, n_hi = (lax.axis_size(axis) for axis in ("aa", "y", "core", "col_hi"))
    n_col = axes_size(COL)
    aa, y, core, col = (lax.axis_index(axis) for axis in ("aa", "y", "core", COL))
    place = jnp.stack([aa, y, core, col]).astype(jnp.int32)
    square, heavy = (rank, rank), 12 * 10**9
    planes = axes_size(PLANE)
    a_parts = (n_aa * n_y, blk_i // (n_y * n_core), rank)
    b_parts = (n_y * n_hi, blk_j // n_hi, rank)
    low = lambda rows: jax.ShapeDtypeStruct((rows, rank), jnp.bfloat16)

    copies = local_call(given_copies_kernel, [(planes, 1, 2 * rank)], b_row, c_row)[0]
    own, other = gather_all(copies, PLANE)
    c_block, partial = local_call(
        first_kernel, [low(blk_k), (n_y * n_core * n_col,) + a_parts[1:]], tensor, own, other, flops=4 * 10**9, place=place
    )
    parts = exchange(partial, ("y", "core") + COL)
    solve, gram_c = local_call(given_kernel, [square, square], own, other, partial, flops=heavy, waits=1)
    own, other = gather_all(local_call(spread_kernel, [a_parts], parts, solve, waits=1)[0], ("aa", "y"))

    raw_a, row, partial = local_call(
        second_kernel,
        [(blk_i, rank), (1, rank), (n_aa * n_col,) + b_parts[1:]],
        tensor, c_block, own, other, solve,
        flops=4 * 10**9, place=place,
    )
    parts = exchange(partial, ("aa",) + COL)
    solve, gram_a, a_low, factor_a = local_call(
        scaled_kernel,
        [square, square, low(blk_i), (1, rank)],
        own, other, solve, gram_c, raw_a, row, partial,
        flops=heavy, waits=1,
    )
    own, other = gather_all(local_call(spread_kernel, [b_parts], parts, solve, waits=1)[0], ("y", "col_hi"))
    raw_b = dot(lax.dynamic_slice_in_dim(own, y * blk_j, blk_j, 0), solve)

    inner = jnp.einsum("ijk,ir->jkr", tensor, a_low, preferred_element_type=F32)
    partial = jnp.sum(inner * raw_b[:, None], axis=0).reshape(blk_k, 1, rank)
    parts = exchange(partial, ("aa", "y", "core"))
    row = lax.dynamic_slice_in_dim(raw_b, aa * n_col + col, 1, 0)
    solve, _, _, factor_b = local_call(
        scaled_kernel,
        [square, square, low(blk_j), (1, rank)],
        own, other, solve, gram_a, raw_b, row, partial,
        flops=heavy, waits=1,
    )

    near, far = ("aa", "core"), ("y",) + COL
    raw_c, squares = local_call(apply_kernel, [(1, rank), (axes_size(near), 1, rank)], parts, solve)
    squares = local_call(spread_kernel, [(axes_size(far), 1, rank)], exchange(squares, near))[0]
    scale = functools.partial(scale_kernel, blk_k * n_col)
    factor_c = local_call(scale, [(1, rank)], exchange(squares, far), raw_c)[0]
    return factor_a, factor_b, factor_c


def solution(mesh):
    n_aa, n_ba, n_col = mesh.devices.shape
    fine = Mesh(
        mesh.devices.reshape(n_aa, n_ba // 2, 2, n_col // 2, 2), ("aa", "y", "core", "col_hi", "col_lo")
    )
    a_spec = P(("aa", "y", "core") + COL, None)
    b_spec = P(("y", "core", "aa") + COL, None)
    c_spec = P(COL + ("aa", "y", "core"), None)
    return jax.shard_map(
        body,
        mesh=fine,
        in_specs=(P("aa", ("y", "core"), COL), b_spec, c_spec),
        out_specs=(a_spec, b_spec, c_spec),
        check_vma=False,
    )
```

```python
import functools

import jax
import jax.numpy as jnp
from jax import lax
from jax.experimental import pallas as pl
from jax.experimental.pallas import tpu as pltpu
from jax.sharding import Mesh, PartitionSpec as P

EPSILON = 1e-06
HIGHEST = lax.Precision.HIGHEST
F32 = jnp.float32


def dot(left, right):
    return jnp.dot(left, right, precision=HIGHEST, preferred_element_type=F32)


def gram_of(rows):
    return lax.dot_general(rows, rows, (((0,), (0,)), ((), ())), precision=HIGHEST, preferred_element_type=F32)


SUB = 8
PANEL = 128
N_COL = 4


def tree_sum(terms):
    while len(terms) > 1:
        terms = [terms[n] + terms[n + 1] if n + 1 < len(terms) else terms[n] for n in range(0, len(terms), 2)]
    return terms[0]


def invert_tile(columns, row_id):
    for k in range(0, SUB, 2):
        a, b = columns[k][k : k + 1, :], columns[k + 1][k : k + 1, :]
        c, d = columns[k][k + 1 : k + 2, :], columns[k + 1][k + 1 : k + 2, :]
        inv = 1.0 / (a * d - b * c)
        first = (d * inv, -b * inv)
        second = (-c * inv, a * inv)
        inside = (row_id == k) | (row_id == k + 1)
        left = jnp.where(row_id == k, -1.0, jnp.where(row_id == k + 1, 0.0, columns[k]))
        right = jnp.where(row_id == k + 1, -1.0, jnp.where(row_id == k, 0.0, columns[k + 1]))
        updated = []
        for j in range(SUB):
            if j in (k, k + 1):
                top, low, base = first[j - k], second[j - k], 0.0
            else:
                x, y = columns[j][k : k + 1, :], columns[j][k + 1 : k + 2, :]
                top, low = first[0] * x + first[1] * y, second[0] * x + second[1] * y
                base = jnp.where(inside, 0.0, columns[j])
            updated.append(base - (left * top + right * low))
        columns = updated
    return columns


def invert_panel(matrix):
    size = matrix.shape[0]
    row_id = lax.broadcasted_iota(jnp.int32, (SUB, size), 0)
    col_id = lax.broadcasted_iota(jnp.int32, (SUB, size), 1)
    tiles = [matrix[lo : lo + SUB, :] for lo in range(0, size, SUB)]
    plain, scaled = [], []
    for q in range(size // SUB):
        lo = q * SUB
        columns = [jnp.broadcast_to(tiles[q][:, lo + j : lo + j + 1], (SUB, size)) for j in range(SUB)]
        columns = invert_tile(columns, row_id)
        inside = (col_id >= lo) & (col_id < lo + SUB)
        pivot = jnp.where(inside, jnp.where(col_id - lo == row_id, 1.0, 0.0), tiles[q])
        rows = tree_sum([columns[j] * pivot[j : j + 1, :] for j in range(SUB)])
        known = col_id < lo + SUB
        plain.append(jnp.where(known, pivot, 0.0))
        scaled.append(jnp.where(known, rows, 0.0))
        for i in range(q + 1, size // SUB):
            tile = tiles[i]
            terms = [tile[:, lo + j : lo + j + 1] * rows[j : j + 1, :] for j in range(SUB)]
            tiles[i] = jnp.where(inside, 0.0, tile) - tree_sum(terms)
    return lax.dot_general(
        jnp.concatenate(plain, axis=0),
        jnp.concatenate(scaled, axis=0),
        (((0,), (0,)), ((), ())),
        precision=HIGHEST,
        preferred_element_type=F32,
    )


def invert_into(matrix, out_ref):
    head = matrix[:PANEL, :PANEL]
    cross = matrix[:PANEL, PANEL:]
    head_inverse = invert_panel(head)
    solved = dot(head_inverse, cross)
    tail_inverse = invert_panel(matrix[PANEL:, PANEL:] - dot(matrix[PANEL:, :PANEL], solved))
    mixed = dot(solved, tail_inverse)
    out_ref[PANEL:, PANEL:] = tail_inverse
    out_ref[:PANEL, PANEL:] = -mixed
    out_ref[PANEL:, :PANEL] = -mixed.T
    out_ref[:PANEL, :PANEL] = head_inverse + lax.dot_general(
        mixed, solved, (((1,), (1,)), ((), ())), precision=HIGHEST, preferred_element_type=F32
    )


ROWS = 8


def one_hot(shape, wanted):
    return jnp.where(lax.broadcasted_iota(jnp.int32, shape, 1) == wanted, 1.0, 0.0)


def first_kernel(place_ref, tensor_ref, own_ref, other_ref, c_block_ref, out_ref):
    y, core, col = place_ref[1], place_ref[2], place_ref[3]
    blk_i, blk_j, blk_k = tensor_ref.shape
    plane, rank = own_ref.shape[0], c_block_ref.shape[1]
    n_col = N_COL
    k = lax.broadcasted_iota(jnp.int32, (blk_k, plane), 0)
    at = k // 16 * (8 * n_col) + k % 16 // 2 * n_col + col
    c_low_own = own_ref[:, rank:].astype(jnp.bfloat16)
    c_low_other = other_ref[:, rank:].astype(jnp.bfloat16)
    mine = k % 2 == core
    pick_own = one_hot((blk_k, plane), jnp.where(mine, at, -1)).astype(jnp.bfloat16)
    pick_other = one_hot((blk_k, plane), jnp.where(mine, -1, at)).astype(jnp.bfloat16)
    c_block = jnp.dot(pick_own, c_low_own, preferred_element_type=F32) + jnp.dot(
        pick_other, c_low_other, preferred_element_type=F32
    )
    c_block = c_block.astype(jnp.bfloat16)
    c_block_ref[...] = c_block
    j = lax.broadcasted_iota(jnp.int32, (blk_j, plane), 0)
    b_block = dot(one_hot((blk_j, plane), j // n_col * (8 * n_col) + y * n_col + j % n_col), own_ref[:, :rank])
    for lo in range(0, blk_i, ROWS):
        flat = tensor_ref[lo : lo + ROWS].reshape(ROWS * blk_j, blk_k)
        inner = jnp.dot(flat, c_block, preferred_element_type=F32)
        for i in range(lo, lo + ROWS):
            row = jnp.sum(inner[(i - lo) * blk_j : (i - lo + 1) * blk_j] * b_block, axis=0, keepdims=True)
            for copy in range(n_col):
                out_ref[i // n_col * n_col + copy, i % n_col : i % n_col + 1, :] = row


def second_kernel(place_ref, tensor_ref, c_block_ref, own_ref, other_ref, solve_ref, raw_ref, row_ref, out_ref):
    aa, y, core, col = place_ref[0], place_ref[1], place_ref[2], place_ref[3]
    blk_i, blk_j, blk_k = tensor_ref.shape
    half = blk_i // 2
    n_col = N_COL
    lo = pl.multiple_of(aa * half, half)
    raw_own = dot(own_ref[pl.ds(lo, half), :], solve_ref[...])
    raw_other = dot(other_ref[pl.ds(lo, half), :], solve_ref[...])
    even = jnp.where(core == 0, raw_own, raw_other)
    odd = jnp.where(core == 0, raw_other, raw_own)
    for step in range(half // n_col):
        raw_ref[2 * step * n_col : (2 * step + 1) * n_col, :] = even[step * n_col : (step + 1) * n_col]
        raw_ref[(2 * step + 1) * n_col : (2 * step + 2) * n_col, :] = odd[step * n_col : (step + 1) * n_col]
    row_ref[...] = raw_ref[pl.ds((2 * y + core) * n_col + col, 1), :]
    c_block = c_block_ref[...]
    total = jnp.zeros((blk_j, row_ref.shape[1]), F32)
    for lo in range(0, blk_i, ROWS):
        flat = tensor_ref[lo : lo + ROWS].reshape(ROWS * blk_j, blk_k)
        inner = jnp.dot(flat, c_block, preferred_element_type=F32)
        for i in range(ROWS):
            total = total + inner[i * blk_j : (i + 1) * blk_j] * raw_ref[lo + i : lo + i + 1, :]
    rows = out_ref.shape[1]
    for dest in range(out_ref.shape[0]):
        lo = dest % n_col * blk_j // n_col // rows * rows
        out_ref[dest] = total[lo : lo + rows]


def given_kernel(own_ref, other_ref, _, inverse_ref, gram_c_ref):
    rank = inverse_ref.shape[0]
    gram_b = gram_of(own_ref[:, :rank]) + gram_of(other_ref[:, :rank])
    gram_c = gram_of(own_ref[:, rank:]) + gram_of(other_ref[:, rank:])
    gram_c_ref[...] = gram_c
    invert_into(gram_b * gram_c, inverse_ref)


def scaled_kernel(
    own_ref, other_ref, solve_ref, other_gram_ref, block_ref, row_ref, _, next_ref, gram_ref, low_ref, out_row_ref
):
    gram = gram_of(dot(own_ref[...], solve_ref[...])) + gram_of(dot(other_ref[...], solve_ref[...]))
    size = gram.shape[0]
    total_rows = 2 * own_ref.shape[0]
    row_id = lax.broadcasted_iota(jnp.int32, (size, size), 0)
    col_id = lax.broadcasted_iota(jnp.int32, (size, size), 1)
    squares = jnp.where(row_id == col_id, gram, 0.0)
    by_col = 1.0 / jnp.sqrt(jnp.sum(squares, axis=0, keepdims=True) / total_rows + EPSILON)
    by_row = 1.0 / jnp.sqrt(jnp.sum(squares, axis=1, keepdims=True) / total_rows + EPSILON)
    gram = gram * by_row * by_col
    low_ref[...] = (block_ref[...] * by_col).astype(low_ref.dtype)
    out_row_ref[...] = row_ref[...] * by_col
    gram_ref[...] = gram
    invert_into(gram * other_gram_ref[...], next_ref)
    next_ref[...] = next_ref[...] * by_row


def spread_kernel(parts_ref, *refs):
    out_ref = refs[-1]
    total = jnp.sum(parts_ref[...], axis=0)
    out_ref[...] = jnp.broadcast_to(total[None], out_ref.shape)


def apply_kernel(parts_ref, solve_ref, raw_ref, squares_ref):
    raw = dot(jnp.sum(parts_ref[...], axis=0), solve_ref[...])
    raw_ref[...] = raw
    squares_ref[...] = jnp.broadcast_to((raw * raw)[None], squares_ref.shape)


def scale_kernel(total_rows, parts_ref, raw_ref, out_ref):
    squares = jnp.sum(parts_ref[...], axis=0)
    out_ref[...] = raw_ref[...] / jnp.sqrt(squares / total_rows + EPSILON)


def local_call(kernel, out_shapes, *operands, flops=10**6, waits=0, place=None):
    vmem = pl.BlockSpec(memory_space=pltpu.VMEM)
    specs = [vmem] * (len(operands) - waits) + [pl.BlockSpec(memory_space=pl.ANY)] * waits
    if place is not None:
        operands, specs = (place,) + operands, [pl.BlockSpec(memory_space=pltpu.SMEM)] + specs
    return pl.pallas_call(
        kernel,
        out_shape=[s if isinstance(s, jax.ShapeDtypeStruct) else jax.ShapeDtypeStruct(s, F32) for s in out_shapes],
        in_specs=specs,
        out_specs=[vmem] * len(out_shapes),
        compiler_params=pltpu.CompilerParams(vmem_limit_bytes=24 * 2**20),
        cost_estimate=pl.CostEstimate(flops=flops, bytes_accessed=2**20, transcendentals=0),
    )(*operands)


def axes_size(axes):
    size = 1
    for axis in axes:
        size *= lax.axis_size(axis)
    return size


def exchange(blocks, axes):
    return lax.all_to_all(blocks, axes, 0, 0, tiled=True)


COL = ("col",)
PLANE = ("aa", "y") + COL


def gather_all(copies, axes):
    own = exchange(copies, axes).reshape(copies.shape[0] * copies.shape[1], copies.shape[2])
    return own, lax.ppermute(own, "core", [(0, 1), (1, 0)])


def body(tensor, b_row, c_row):
    blk_i, blk_j, blk_k = tensor.shape
    rank = b_row.shape[1]
    n_aa, n_y, n_core, n_col = (lax.axis_size(axis) for axis in ("aa", "y", "core", "col"))
    aa, y, core, col = (lax.axis_index(axis) for axis in ("aa", "y", "core", COL))
    place = jnp.stack([aa, y, core, col]).astype(jnp.int32)
    square, heavy = (rank, rank), 12 * 10**9
    planes = axes_size(PLANE)
    a_parts = (n_aa * n_y, blk_i // (n_y * n_core), rank)
    b_parts = (n_y * n_col, blk_j // n_col, rank)
    low = lambda rows: jax.ShapeDtypeStruct((rows, rank), jnp.bfloat16)

    given = jnp.concatenate([b_row, c_row], axis=1)[None]
    own, other = gather_all(jnp.broadcast_to(given, (planes, 1, 2 * rank)), PLANE)
    c_block, partial = local_call(
        first_kernel, [low(blk_k), (n_y * n_core * n_col,) + a_parts[1:]], tensor, own, other, flops=4 * 10**9, place=place
    )
    parts = exchange(partial, ("y", "core") + COL)
    solve, gram_c = local_call(given_kernel, [square, square], own, other, partial, flops=heavy, waits=1)
    own, other = gather_all(local_call(spread_kernel, [a_parts], parts, solve, waits=1)[0], ("aa", "y"))

    raw_a, row, partial = local_call(
        second_kernel,
        [(blk_i, rank), (1, rank), (n_aa * n_col,) + b_parts[1:]],
        tensor, c_block, own, other, solve,
        flops=4 * 10**9, place=place,
    )
    parts = exchange(partial, ("aa",) + COL)
    solve, gram_a, a_low, factor_a = local_call(
        scaled_kernel,
        [square, square, low(blk_i), (1, rank)],
        own, other, solve, gram_c, raw_a, row, partial,
        flops=heavy, waits=1,
    )
    own, other = gather_all(local_call(spread_kernel, [b_parts], parts, solve, waits=1)[0], ("y",) + COL)
    raw_b = dot(lax.dynamic_slice_in_dim(own, y * blk_j, blk_j, 0), solve)

    inner = jnp.einsum("ijk,ir->jkr", tensor, a_low, preferred_element_type=F32)
    partial = jnp.sum(inner * raw_b[:, None], axis=0).reshape(blk_k, 1, rank)
    parts = exchange(partial, ("aa", "y", "core"))
    row = lax.dynamic_slice_in_dim(raw_b, aa * n_col + col, 1, 0)
    solve, _, _, factor_b = local_call(
        scaled_kernel,
        [square, square, low(blk_j), (1, rank)],
        own, other, solve, gram_a, raw_b, row, partial,
        flops=heavy, waits=1,
    )

    near, far = ("aa", "core"), ("y",) + COL
    raw_c, squares = local_call(apply_kernel, [(1, rank), (axes_size(near), 1, rank)], parts, solve)
    squares = local_call(spread_kernel, [(axes_size(far), 1, rank)], exchange(squares, near))[0]
    scale = functools.partial(scale_kernel, blk_k * n_col)
    factor_c = local_call(scale, [(1, rank)], exchange(squares, far), raw_c)[0]
    return factor_a, factor_b, factor_c


def solution(mesh):
    n_aa, n_ba, n_col = mesh.devices.shape
    fine = Mesh(mesh.devices.reshape(n_aa, n_ba // 2, 2, n_col), ("aa", "y", "core", "col"))
    a_spec = P(("aa", "y", "core") + COL, None)
    b_spec = P(("y", "core", "aa") + COL, None)
    c_spec = P(COL + ("aa", "y", "core"), None)
    return jax.shard_map(
        body,
        mesh=fine,
        in_specs=(P("aa", ("y", "core"), COL), b_spec, c_spec),
        out_specs=(a_spec, b_spec, c_spec),
        check_vma=False,
    )
```

```python
import functools

import jax
import jax.numpy as jnp
from jax import lax
from jax.experimental import pallas as pl
from jax.experimental.pallas import tpu as pltpu
from jax.sharding import Mesh, PartitionSpec as P

EPSILON = 1e-06
HIGHEST = lax.Precision.HIGHEST
F32 = jnp.float32


def dot(left, right):
    return jnp.dot(left, right, precision=HIGHEST, preferred_element_type=F32)


def gram_of(rows):
    return lax.dot_general(rows, rows, (((0,), (0,)), ((), ())), precision=HIGHEST, preferred_element_type=F32)


SUB = 8
PANEL = 128
N_COL = 4


def tree_sum(terms):
    while len(terms) > 1:
        terms = [terms[n] + terms[n + 1] if n + 1 < len(terms) else terms[n] for n in range(0, len(terms), 2)]
    return terms[0]


def invert_tile(columns, row_id):
    for k in range(0, SUB, 2):
        a, b = columns[k][k : k + 1, :], columns[k + 1][k : k + 1, :]
        c, d = columns[k][k + 1 : k + 2, :], columns[k + 1][k + 1 : k + 2, :]
        inv = 1.0 / (a * d - b * c)
        first = (d * inv, -b * inv)
        second = (-c * inv, a * inv)
        inside = (row_id == k) | (row_id == k + 1)
        left = jnp.where(row_id == k, -1.0, jnp.where(row_id == k + 1, 0.0, columns[k]))
        right = jnp.where(row_id == k + 1, -1.0, jnp.where(row_id == k, 0.0, columns[k + 1]))
        updated = []
        for j in range(SUB):
            if j in (k, k + 1):
                top, low, base = first[j - k], second[j - k], 0.0
            else:
                x, y = columns[j][k : k + 1, :], columns[j][k + 1 : k + 2, :]
                top, low = first[0] * x + first[1] * y, second[0] * x + second[1] * y
                base = jnp.where(inside, 0.0, columns[j])
            updated.append(base - (left * top + right * low))
        columns = updated
    return columns


def invert_panel(matrix):
    size = matrix.shape[0]
    row_id = lax.broadcasted_iota(jnp.int32, (SUB, size), 0)
    col_id = lax.broadcasted_iota(jnp.int32, (SUB, size), 1)
    tiles = [matrix[lo : lo + SUB, :] for lo in range(0, size, SUB)]
    plain, scaled = [], []
    for q in range(size // SUB):
        lo = q * SUB
        columns = [jnp.broadcast_to(tiles[q][:, lo + j : lo + j + 1], (SUB, size)) for j in range(SUB)]
        columns = invert_tile(columns, row_id)
        inside = (col_id >= lo) & (col_id < lo + SUB)
        pivot = jnp.where(inside, jnp.where(col_id - lo == row_id, 1.0, 0.0), tiles[q])
        rows = tree_sum([columns[j] * pivot[j : j + 1, :] for j in range(SUB)])
        known = col_id < lo + SUB
        plain.append(jnp.where(known, pivot, 0.0))
        scaled.append(jnp.where(known, rows, 0.0))
        for i in range(q + 1, size // SUB):
            tile = tiles[i]
            terms = [tile[:, lo + j : lo + j + 1] * rows[j : j + 1, :] for j in range(SUB)]
            tiles[i] = jnp.where(inside, 0.0, tile) - tree_sum(terms)
    return lax.dot_general(
        jnp.concatenate(plain, axis=0),
        jnp.concatenate(scaled, axis=0),
        (((0,), (0,)), ((), ())),
        precision=HIGHEST,
        preferred_element_type=F32,
    )


def invert_into(matrix, out_ref):
    head = matrix[:PANEL, :PANEL]
    cross = matrix[:PANEL, PANEL:]
    head_inverse = invert_panel(head)
    solved = dot(head_inverse, cross)
    tail_inverse = invert_panel(matrix[PANEL:, PANEL:] - dot(matrix[PANEL:, :PANEL], solved))
    mixed = dot(solved, tail_inverse)
    out_ref[PANEL:, PANEL:] = tail_inverse
    out_ref[:PANEL, PANEL:] = -mixed
    out_ref[PANEL:, :PANEL] = -mixed.T
    out_ref[:PANEL, :PANEL] = head_inverse + lax.dot_general(
        mixed, solved, (((1,), (1,)), ((), ())), precision=HIGHEST, preferred_element_type=F32
    )


ROWS = 8


def one_hot(shape, wanted):
    return jnp.where(lax.broadcasted_iota(jnp.int32, shape, 1) == wanted, 1.0, 0.0)


def first_kernel(place_ref, tensor_ref, own_ref, other_ref, c_block_ref, out_ref):
    y, core, col = place_ref[1], place_ref[2], place_ref[3]
    blk_i, blk_j, blk_k = tensor_ref.shape
    plane, rank = own_ref.shape[0], c_block_ref.shape[1]
    n_col = N_COL
    k = lax.broadcasted_iota(jnp.int32, (blk_k, plane), 0)
    at = k // 16 * (8 * n_col) + k % 16 // 2 * n_col + col
    c_low_own = own_ref[:, rank:].astype(jnp.bfloat16)
    c_low_other = other_ref[:, rank:].astype(jnp.bfloat16)
    mine = k % 2 == core
    pick_own = one_hot((blk_k, plane), jnp.where(mine, at, -1)).astype(jnp.bfloat16)
    pick_other = one_hot((blk_k, plane), jnp.where(mine, -1, at)).astype(jnp.bfloat16)
    c_block = jnp.dot(pick_own, c_low_own, preferred_element_type=F32) + jnp.dot(
        pick_other, c_low_other, preferred_element_type=F32
    )
    c_block = c_block.astype(jnp.bfloat16)
    c_block_ref[...] = c_block
    j = lax.broadcasted_iota(jnp.int32, (blk_j, plane), 0)
    b_block = dot(one_hot((blk_j, plane), j // n_col * (8 * n_col) + y * n_col + j % n_col), own_ref[:, :rank])
    for lo in range(0, blk_i, ROWS):
        flat = tensor_ref[lo : lo + ROWS].reshape(ROWS * blk_j, blk_k)
        inner = jnp.dot(flat, c_block, preferred_element_type=F32)
        rows = [
            jnp.sum(inner[i * blk_j : (i + 1) * blk_j] * b_block, axis=0, keepdims=True) for i in range(ROWS)
        ]
        for i in range(0, ROWS, n_col):
            group = jnp.concatenate(rows[i : i + n_col], axis=0)
            for copy in range(n_col):
                out_ref[lo + i + copy] = group


def second_kernel(place_ref, tensor_ref, c_block_ref, own_ref, other_ref, solve_ref, raw_ref, row_ref, out_ref):
    aa, y, core, col = place_ref[0], place_ref[1], place_ref[2], place_ref[3]
    blk_i, blk_j, blk_k = tensor_ref.shape
    half = blk_i // 2
    n_col = N_COL
    lo = pl.multiple_of(aa * half, half)
    raw_own = dot(own_ref[pl.ds(lo, half), :], solve_ref[...])
    raw_other = dot(other_ref[pl.ds(lo, half), :], solve_ref[...])
    even = jnp.where(core == 0, raw_own, raw_other)
    odd = jnp.where(core == 0, raw_other, raw_own)
    for step in range(half // n_col):
        raw_ref[2 * step * n_col : (2 * step + 1) * n_col, :] = even[step * n_col : (step + 1) * n_col]
        raw_ref[(2 * step + 1) * n_col : (2 * step + 2) * n_col, :] = odd[step * n_col : (step + 1) * n_col]
    row_ref[...] = raw_ref[pl.ds((2 * y + core) * n_col + col, 1), :]
    c_block = c_block_ref[...]
    total = jnp.zeros((blk_j, row_ref.shape[1]), F32)
    for lo in range(0, blk_i, ROWS):
        flat = tensor_ref[lo : lo + ROWS].reshape(ROWS * blk_j, blk_k)
        inner = jnp.dot(flat, c_block, preferred_element_type=F32)
        for i in range(ROWS):
            total = total + inner[i * blk_j : (i + 1) * blk_j] * raw_ref[lo + i : lo + i + 1, :]
    rows = out_ref.shape[1]
    for dest in range(out_ref.shape[0]):
        lo = dest % n_col * blk_j // n_col // rows * rows
        out_ref[dest] = total[lo : lo + rows]


def given_kernel(own_ref, other_ref, _, inverse_ref, gram_c_ref):
    rank = inverse_ref.shape[0]
    gram_b = gram_of(own_ref[:, :rank]) + gram_of(other_ref[:, :rank])
    gram_c = gram_of(own_ref[:, rank:]) + gram_of(other_ref[:, rank:])
    gram_c_ref[...] = gram_c
    invert_into(gram_b * gram_c, inverse_ref)


def scaled_kernel(
    own_ref, other_ref, solve_ref, other_gram_ref, block_ref, row_ref, _, next_ref, gram_ref, low_ref, out_row_ref
):
    gram = gram_of(dot(own_ref[...], solve_ref[...])) + gram_of(dot(other_ref[...], solve_ref[...]))
    size = gram.shape[0]
    total_rows = 2 * own_ref.shape[0]
    row_id = lax.broadcasted_iota(jnp.int32, (size, size), 0)
    col_id = lax.broadcasted_iota(jnp.int32, (size, size), 1)
    squares = jnp.where(row_id == col_id, gram, 0.0)
    by_col = 1.0 / jnp.sqrt(jnp.sum(squares, axis=0, keepdims=True) / total_rows + EPSILON)
    by_row = 1.0 / jnp.sqrt(jnp.sum(squares, axis=1, keepdims=True) / total_rows + EPSILON)
    gram = gram * by_row * by_col
    low_ref[...] = (block_ref[...] * by_col).astype(low_ref.dtype)
    out_row_ref[...] = row_ref[...] * by_col
    gram_ref[...] = gram
    invert_into(gram * other_gram_ref[...], next_ref)
    next_ref[...] = next_ref[...] * by_row


def spread_kernel(parts_ref, *refs):
    out_ref = refs[-1]
    total = jnp.sum(parts_ref[...], axis=0)
    out_ref[...] = jnp.broadcast_to(total[None], out_ref.shape)


def apply_kernel(parts_ref, solve_ref, raw_ref, squares_ref):
    raw = dot(jnp.sum(parts_ref[...], axis=0), solve_ref[...])
    raw_ref[...] = raw
    squares_ref[...] = jnp.broadcast_to((raw * raw)[None], squares_ref.shape)


def scale_kernel(total_rows, parts_ref, raw_ref, out_ref):
    squares = jnp.sum(parts_ref[...], axis=0)
    out_ref[...] = raw_ref[...] / jnp.sqrt(squares / total_rows + EPSILON)


def local_call(kernel, out_shapes, *operands, flops=10**6, waits=0, place=None):
    vmem = pl.BlockSpec(memory_space=pltpu.VMEM)
    specs = [vmem] * (len(operands) - waits) + [pl.BlockSpec(memory_space=pl.ANY)] * waits
    if place is not None:
        operands, specs = (place,) + operands, [pl.BlockSpec(memory_space=pltpu.SMEM)] + specs
    return pl.pallas_call(
        kernel,
        out_shape=[s if isinstance(s, jax.ShapeDtypeStruct) else jax.ShapeDtypeStruct(s, F32) for s in out_shapes],
        in_specs=specs,
        out_specs=[vmem] * len(out_shapes),
        compiler_params=pltpu.CompilerParams(vmem_limit_bytes=24 * 2**20),
        cost_estimate=pl.CostEstimate(flops=flops, bytes_accessed=2**20, transcendentals=0),
    )(*operands)


def axes_size(axes):
    size = 1
    for axis in axes:
        size *= lax.axis_size(axis)
    return size


def exchange(blocks, axes):
    return lax.all_to_all(blocks, axes, 0, 0, tiled=True)


COL = ("col",)
PLANE = ("aa", "y") + COL


def gather_all(copies, axes):
    own = exchange(copies, axes).reshape(copies.shape[0] * copies.shape[1], copies.shape[2])
    return own, lax.ppermute(own, "core", [(0, 1), (1, 0)])


def body(tensor, b_row, c_row):
    blk_i, blk_j, blk_k = tensor.shape
    rank = b_row.shape[1]
    n_aa, n_y, n_core, n_col = (lax.axis_size(axis) for axis in ("aa", "y", "core", "col"))
    aa, y, core, col = (lax.axis_index(axis) for axis in ("aa", "y", "core", COL))
    place = jnp.stack([aa, y, core, col]).astype(jnp.int32)
    square, heavy = (rank, rank), 12 * 10**9
    planes = axes_size(PLANE)
    a_parts = (n_aa * n_y, blk_i // (n_y * n_core), rank)
    b_parts = (n_y * n_col, blk_j // n_col, rank)
    low = lambda rows: jax.ShapeDtypeStruct((rows, rank), jnp.bfloat16)

    given = jnp.concatenate([b_row, c_row], axis=1)[None]
    own, other = gather_all(jnp.broadcast_to(given, (planes, 1, 2 * rank)), PLANE)
    c_block, partial = local_call(
        first_kernel, [low(blk_k), (n_y * n_core * n_col,) + a_parts[1:]], tensor, own, other, flops=4 * 10**9, place=place
    )
    parts = exchange(partial, ("y", "core") + COL)
    solve, gram_c = local_call(given_kernel, [square, square], own, other, partial, flops=heavy, waits=1)
    own, other = gather_all(local_call(spread_kernel, [a_parts], parts, solve, waits=1)[0], ("aa", "y"))

    raw_a, row, partial = local_call(
        second_kernel,
        [(blk_i, rank), (1, rank), (n_aa * n_col,) + b_parts[1:]],
        tensor, c_block, own, other, solve,
        flops=4 * 10**9, place=place,
    )
    parts = exchange(partial, ("aa",) + COL)
    solve, gram_a, a_low, factor_a = local_call(
        scaled_kernel,
        [square, square, low(blk_i), (1, rank)],
        own, other, solve, gram_c, raw_a, row, partial,
        flops=heavy, waits=1,
    )
    own, other = gather_all(local_call(spread_kernel, [b_parts], parts, solve, waits=1)[0], ("y",) + COL)
    raw_b = dot(lax.dynamic_slice_in_dim(own, y * blk_j, blk_j, 0), solve)

    inner = jnp.einsum("ijk,ir->jkr", tensor, a_low, preferred_element_type=F32)
    partial = jnp.sum(inner * raw_b[:, None], axis=0).reshape(blk_k, 1, rank)
    parts = exchange(partial, ("aa", "y", "core"))
    row = lax.dynamic_slice_in_dim(raw_b, aa * n_col + col, 1, 0)
    solve, _, _, factor_b = local_call(
        scaled_kernel,
        [square, square, low(blk_j), (1, rank)],
        own, other, solve, gram_a, raw_b, row, partial,
        flops=heavy, waits=1,
    )

    near, far = ("y",) + COL, ("aa", "core")
    raw_c, squares = local_call(apply_kernel, [(1, rank), (axes_size(near), 1, rank)], parts, solve)
    squares = local_call(spread_kernel, [(axes_size(far), 1, rank)], exchange(squares, near))[0]
    scale = functools.partial(scale_kernel, blk_k * n_col)
    factor_c = local_call(scale, [(1, rank)], exchange(squares, far), raw_c)[0]
    return factor_a, factor_b, factor_c


def solution(mesh):
    n_aa, n_ba, n_col = mesh.devices.shape
    fine = Mesh(mesh.devices.reshape(n_aa, n_ba // 2, 2, n_col), ("aa", "y", "core", "col"))
    a_spec = P(("aa", "y", "core") + COL, None)
    b_spec = P(("y", "core", "aa") + COL, None)
    c_spec = P(COL + ("aa", "y", "core"), None)
    return jax.shard_map(
        body,
        mesh=fine,
        in_specs=(P("aa", ("y", "core"), COL), b_spec, c_spec),
        out_specs=(a_spec, b_spec, c_spec),
        check_vma=False,
    )
```

```python
import functools

import jax
import jax.numpy as jnp
from jax import lax
from jax.experimental import pallas as pl
from jax.experimental.pallas import tpu as pltpu
from jax.sharding import Mesh, PartitionSpec as P

EPSILON = 1e-06
HIGHEST = lax.Precision.HIGHEST
F32 = jnp.float32


def dot(left, right):
    return jnp.dot(left, right, precision=HIGHEST, preferred_element_type=F32)


def gram_of(rows):
    return lax.dot_general(rows, rows, (((0,), (0,)), ((), ())), precision=HIGHEST, preferred_element_type=F32)


SUB = 8
PANEL = 128
N_COL = 4


def tree_sum(terms):
    while len(terms) > 1:
        terms = [terms[n] + terms[n + 1] if n + 1 < len(terms) else terms[n] for n in range(0, len(terms), 2)]
    return terms[0]


def invert_tile(columns, row_id):
    for k in range(0, SUB, 2):
        a, b = columns[k][k : k + 1, :], columns[k + 1][k : k + 1, :]
        c, d = columns[k][k + 1 : k + 2, :], columns[k + 1][k + 1 : k + 2, :]
        inv = 1.0 / (a * d - b * c)
        first = (d * inv, -b * inv)
        second = (-c * inv, a * inv)
        inside = (row_id == k) | (row_id == k + 1)
        left = jnp.where(row_id == k, -1.0, jnp.where(row_id == k + 1, 0.0, columns[k]))
        right = jnp.where(row_id == k + 1, -1.0, jnp.where(row_id == k, 0.0, columns[k + 1]))
        updated = []
        for j in range(SUB):
            if j in (k, k + 1):
                top, low, base = first[j - k], second[j - k], 0.0
            else:
                x, y = columns[j][k : k + 1, :], columns[j][k + 1 : k + 2, :]
                top, low = first[0] * x + first[1] * y, second[0] * x + second[1] * y
                base = jnp.where(inside, 0.0, columns[j])
            updated.append(base - (left * top + right * low))
        columns = updated
    return columns


def invert_panel(matrix):
    size = matrix.shape[0]
    row_id = lax.broadcasted_iota(jnp.int32, (SUB, size), 0)
    col_id = lax.broadcasted_iota(jnp.int32, (SUB, size), 1)
    tiles = [matrix[lo : lo + SUB, :] for lo in range(0, size, SUB)]
    plain, scaled = [], []
    for q in range(size // SUB):
        lo = q * SUB
        columns = [jnp.broadcast_to(tiles[q][:, lo + j : lo + j + 1], (SUB, size)) for j in range(SUB)]
        columns = invert_tile(columns, row_id)
        inside = (col_id >= lo) & (col_id < lo + SUB)
        pivot = jnp.where(inside, jnp.where(col_id - lo == row_id, 1.0, 0.0), tiles[q])
        rows = tree_sum([columns[j] * pivot[j : j + 1, :] for j in range(SUB)])
        known = col_id < lo + SUB
        plain.append(jnp.where(known, pivot, 0.0))
        scaled.append(jnp.where(known, rows, 0.0))
        for i in range(q + 1, size // SUB):
            tile = tiles[i]
            terms = [tile[:, lo + j : lo + j + 1] * rows[j : j + 1, :] for j in range(SUB)]
            tiles[i] = jnp.where(inside, 0.0, tile) - tree_sum(terms)
    return lax.dot_general(
        jnp.concatenate(plain, axis=0),
        jnp.concatenate(scaled, axis=0),
        (((0,), (0,)), ((), ())),
        precision=HIGHEST,
        preferred_element_type=F32,
    )


def invert_into(matrix, out_ref):
    head = matrix[:PANEL, :PANEL]
    cross = matrix[:PANEL, PANEL:]
    head_inverse = invert_panel(head)
    solved = dot(head_inverse, cross)
    tail_inverse = invert_panel(matrix[PANEL:, PANEL:] - dot(matrix[PANEL:, :PANEL], solved))
    mixed = dot(solved, tail_inverse)
    out_ref[PANEL:, PANEL:] = tail_inverse
    out_ref[:PANEL, PANEL:] = -mixed
    out_ref[PANEL:, :PANEL] = -mixed.T
    out_ref[:PANEL, :PANEL] = head_inverse + lax.dot_general(
        mixed, solved, (((1,), (1,)), ((), ())), precision=HIGHEST, preferred_element_type=F32
    )


ROWS = 8


def one_hot(shape, wanted):
    return jnp.where(lax.broadcasted_iota(jnp.int32, shape, 1) == wanted, 1.0, 0.0)


def first_kernel(place_ref, tensor_ref, own_ref, other_ref, c_block_ref, out_ref):
    y, core, col = place_ref[1], place_ref[2], place_ref[3]
    blk_i, blk_j, blk_k = tensor_ref.shape
    plane, rank = own_ref.shape[0], c_block_ref.shape[1]
    n_col = N_COL
    k = lax.broadcasted_iota(jnp.int32, (blk_k, plane), 0)
    at = k // 16 * (8 * n_col) + k % 16 // 2 * n_col + col
    c_low_own = own_ref[:, rank:].astype(jnp.bfloat16)
    c_low_other = other_ref[:, rank:].astype(jnp.bfloat16)
    mine = k % 2 == core
    pick_own = one_hot((blk_k, plane), jnp.where(mine, at, -1)).astype(jnp.bfloat16)
    pick_other = one_hot((blk_k, plane), jnp.where(mine, -1, at)).astype(jnp.bfloat16)
    c_block = jnp.dot(pick_own, c_low_own, preferred_element_type=F32) + jnp.dot(
        pick_other, c_low_other, preferred_element_type=F32
    )
    c_block = c_block.astype(jnp.bfloat16)
    c_block_ref[...] = c_block
    j = lax.broadcasted_iota(jnp.int32, (blk_j, plane), 0)
    b_block = dot(one_hot((blk_j, plane), j // n_col * (8 * n_col) + y * n_col + j % n_col), own_ref[:, :rank])
    for lo in range(0, blk_i, ROWS):
        flat = tensor_ref[lo : lo + ROWS].reshape(ROWS * blk_j, blk_k)
        inner = jnp.dot(flat, c_block, preferred_element_type=F32)
        rows = [
            jnp.sum(inner[i * blk_j : (i + 1) * blk_j] * b_block, axis=0, keepdims=True) for i in range(ROWS)
        ]
        for i in range(0, ROWS, n_col):
            group = jnp.concatenate(rows[i : i + n_col], axis=0)
            for copy in range(n_col):
                out_ref[lo + i + copy] = group


def second_kernel(place_ref, tensor_ref, c_block_ref, own_ref, other_ref, solve_ref, raw_ref, row_ref, out_ref):
    aa, y, core, col = place_ref[0], place_ref[1], place_ref[2], place_ref[3]
    blk_i, blk_j, blk_k = tensor_ref.shape
    half = blk_i // 2
    n_col = N_COL
    lo = pl.multiple_of(aa * half, half)
    raw_own = dot(own_ref[pl.ds(lo, half), :], solve_ref[...])
    raw_other = dot(other_ref[pl.ds(lo, half), :], solve_ref[...])
    even = jnp.where(core == 0, raw_own, raw_other)
    odd = jnp.where(core == 0, raw_other, raw_own)
    for step in range(half // n_col):
        raw_ref[2 * step * n_col : (2 * step + 1) * n_col, :] = even[step * n_col : (step + 1) * n_col]
        raw_ref[(2 * step + 1) * n_col : (2 * step + 2) * n_col, :] = odd[step * n_col : (step + 1) * n_col]
    row_ref[...] = raw_ref[pl.ds((2 * y + core) * n_col + col, 1), :]
    c_block = c_block_ref[...]
    total = jnp.zeros((blk_j, row_ref.shape[1]), F32)
    for lo in range(0, blk_i, ROWS):
        flat = tensor_ref[lo : lo + ROWS].reshape(ROWS * blk_j, blk_k)
        inner = jnp.dot(flat, c_block, preferred_element_type=F32)
        for i in range(ROWS):
            total = total + inner[i * blk_j : (i + 1) * blk_j] * raw_ref[lo + i : lo + i + 1, :]
    rows = out_ref.shape[1]
    for dest in range(out_ref.shape[0]):
        lo = dest % n_col * blk_j // n_col // rows * rows
        out_ref[dest] = total[lo : lo + rows]


def given_kernel(own_ref, other_ref, _, inverse_ref, gram_c_ref):
    rank = inverse_ref.shape[0]
    gram_b = gram_of(own_ref[:, :rank]) + gram_of(other_ref[:, :rank])
    gram_c = gram_of(own_ref[:, rank:]) + gram_of(other_ref[:, rank:])
    gram_c_ref[...] = gram_c
    invert_into(gram_b * gram_c, inverse_ref)


def scaled_kernel(
    own_ref, other_ref, solve_ref, other_gram_ref, block_ref, row_ref, _, next_ref, gram_ref, low_ref, out_row_ref
):
    gram = gram_of(dot(own_ref[...], solve_ref[...])) + gram_of(dot(other_ref[...], solve_ref[...]))
    size = gram.shape[0]
    total_rows = 2 * own_ref.shape[0]
    row_id = lax.broadcasted_iota(jnp.int32, (size, size), 0)
    col_id = lax.broadcasted_iota(jnp.int32, (size, size), 1)
    squares = jnp.where(row_id == col_id, gram, 0.0)
    by_col = 1.0 / jnp.sqrt(jnp.sum(squares, axis=0, keepdims=True) / total_rows + EPSILON)
    by_row = 1.0 / jnp.sqrt(jnp.sum(squares, axis=1, keepdims=True) / total_rows + EPSILON)
    gram = gram * by_row * by_col
    low_ref[...] = (block_ref[...] * by_col).astype(low_ref.dtype)
    out_row_ref[...] = row_ref[...] * by_col
    gram_ref[...] = gram
    invert_into(gram * other_gram_ref[...], next_ref)
    next_ref[...] = next_ref[...] * by_row


def spread_kernel(parts_ref, *refs):
    out_ref = refs[-1]
    total = jnp.sum(parts_ref[...], axis=0)
    out_ref[...] = jnp.broadcast_to(total[None], out_ref.shape)


def apply_kernel(parts_ref, solve_ref, raw_ref, squares_ref):
    raw = dot(jnp.sum(parts_ref[...], axis=0), solve_ref[...])
    raw_ref[...] = raw
    squares_ref[...] = jnp.broadcast_to((raw * raw)[None], squares_ref.shape)


def scale_kernel(total_rows, parts_ref, raw_ref, out_ref):
    squares = jnp.sum(parts_ref[...], axis=0)
    out_ref[...] = raw_ref[...] / jnp.sqrt(squares / total_rows + EPSILON)


def local_call(kernel, out_shapes, *operands, flops=10**6, waits=0, place=None):
    vmem = pl.BlockSpec(memory_space=pltpu.VMEM)
    specs = [vmem] * (len(operands) - waits) + [pl.BlockSpec(memory_space=pl.ANY)] * waits
    if place is not None:
        operands, specs = (place,) + operands, [pl.BlockSpec(memory_space=pltpu.SMEM)] + specs
    return pl.pallas_call(
        kernel,
        out_shape=[s if isinstance(s, jax.ShapeDtypeStruct) else jax.ShapeDtypeStruct(s, F32) for s in out_shapes],
        in_specs=specs,
        out_specs=[vmem] * len(out_shapes),
        compiler_params=pltpu.CompilerParams(vmem_limit_bytes=24 * 2**20),
        cost_estimate=pl.CostEstimate(flops=flops, bytes_accessed=2**20, transcendentals=0),
    )(*operands)


def axes_size(axes):
    size = 1
    for axis in axes:
        size *= lax.axis_size(axis)
    return size


def exchange(blocks, axes):
    return lax.all_to_all(blocks, axes, 0, 0, tiled=True)


COL = ("col",)
PLANE = ("aa", "y") + COL


def gather_all(copies, axes):
    own = exchange(copies, axes).reshape(copies.shape[0] * copies.shape[1], copies.shape[2])
    return own, lax.ppermute(own, "core", [(0, 1), (1, 0)])


def body(tensor, b_row, c_row):
    blk_i, blk_j, blk_k = tensor.shape
    rank = b_row.shape[1]
    n_aa, n_y, n_core, n_col = (lax.axis_size(axis) for axis in ("aa", "y", "core", "col"))
    aa, y, core, col = (lax.axis_index(axis) for axis in ("aa", "y", "core", COL))
    place = jnp.stack([aa, y, core, col]).astype(jnp.int32)
    square, heavy = (rank, rank), 12 * 10**9
    planes = axes_size(PLANE)
    a_parts = (n_aa * n_y, blk_i // (n_y * n_core), rank)
    b_parts = (n_y * n_col, blk_j // n_col, rank)
    low = lambda rows: jax.ShapeDtypeStruct((rows, rank), jnp.bfloat16)

    given = jnp.concatenate([b_row, c_row], axis=1)[None]
    own, other = gather_all(jnp.broadcast_to(given, (planes, 1, 2 * rank)), PLANE)
    c_block, partial = local_call(
        first_kernel, [low(blk_k), (n_y * n_core * n_col,) + a_parts[1:]], tensor, own, other, flops=4 * 10**9, place=place
    )
    parts = exchange(partial, ("y", "core") + COL)
    solve, gram_c = local_call(given_kernel, [square, square], own, other, partial, flops=heavy, waits=1)
    own, other = gather_all(local_call(spread_kernel, [a_parts], parts, solve, waits=1)[0], ("aa", "y"))

    raw_a, row, partial = local_call(
        second_kernel,
        [(blk_i, rank), (1, rank), (n_aa * n_col,) + b_parts[1:]],
        tensor, c_block, own, other, solve,
        flops=4 * 10**9, place=place,
    )
    parts = exchange(partial, ("aa",) + COL)
    solve, gram_a, a_low, factor_a = local_call(
        scaled_kernel,
        [square, square, low(blk_i), (1, rank)],
        own, other, solve, gram_c, raw_a, row, partial,
        flops=heavy, waits=1,
    )
    own, other = gather_all(local_call(spread_kernel, [b_parts], parts, solve, waits=1)[0], ("y",) + COL)
    raw_b = dot(lax.dynamic_slice_in_dim(own, y * blk_j, blk_j, 0), solve)

    inner = jnp.einsum("ijk,ir->jkr", tensor, a_low, preferred_element_type=F32)
    partial = jnp.sum(inner * raw_b[:, None], axis=0).reshape(blk_k, 1, rank)
    parts = exchange(partial, ("aa", "y", "core"))
    row = lax.dynamic_slice_in_dim(raw_b, aa * n_col + col, 1, 0)
    solve, _, _, factor_b = local_call(
        scaled_kernel,
        [square, square, low(blk_j), (1, rank)],
        own, other, solve, gram_a, raw_b, row, partial,
        flops=heavy, waits=1,
    )

    near, far = ("aa", "y"), ("core",) + COL
    raw_c, squares = local_call(apply_kernel, [(1, rank), (axes_size(near), 1, rank)], parts, solve)
    squares = local_call(spread_kernel, [(axes_size(far), 1, rank)], exchange(squares, near))[0]
    scale = functools.partial(scale_kernel, blk_k * n_col)
    factor_c = local_call(scale, [(1, rank)], exchange(squares, far), raw_c)[0]
    return factor_a, factor_b, factor_c


def solution(mesh):
    n_aa, n_ba, n_col = mesh.devices.shape
    fine = Mesh(mesh.devices.reshape(n_aa, n_ba // 2, 2, n_col), ("aa", "y", "core", "col"))
    a_spec = P(("aa", "y", "core") + COL, None)
    b_spec = P(("y", "core", "aa") + COL, None)
    c_spec = P(COL + ("aa", "y", "core"), None)
    return jax.shard_map(
        body,
        mesh=fine,
        in_specs=(P("aa", ("y", "core"), COL), b_spec, c_spec),
        out_specs=(a_spec, b_spec, c_spec),
        check_vma=False,
    )
```
